32 devices in a mesh: row: 8 (over z, x), grp: 4 (over y, core).
Axes of the slice: x: 2, y: 2, z: 4, core: 2. Of those that a mesh axis runs over, the one named last changes fastest.
Arguments:
- features: bfloat16 [65536, 768], P(('row', 'grp')), may hold values from -6 to 6
- dense_edge_weights: bfloat16 [256, 4, 256, 256], P(('row', 'grp')), may hold values from -0.15625 to 0.15625
- dense_cols: int32 [256, 4], P(('row', 'grp')), may hold values from 0 to 7
- dense_ids: int32 [8], replicated, may hold values from 0 to 255, as said below
- sparse_w: bfloat16 [65536, 256], P(('row', 'grp')), may hold values from -0.15625 to 0.15625
- sparse_rows: int32 [32, 32, 8], P(('row', 'grp')), may hold values from 0 to 2047, as said below
- sparse_counts: int32 [32, 32], P(('row', 'grp')), may hold values from 1 to 8, as said below
- weight: bfloat16 [768, 768], replicated, may hold values from -0.21875 to 0.21875
- bias: float32 [768], replicated, may hold values from -3 to 3
Outputs:
- output: bfloat16 [65536, 768], P(('row', 'grp'))
The draws below stay inside these ranges and needn't reach their ends.
Inputs may be any that keep to these rules, and one draw needn't show every extreme that they name: `dense_ids`: distinct row block ids; the first and the last row block are both among them. `sparse_rows`: local row indices of the sender. `sparse_counts`: at most 8 rows from one sender to one receiver; one receiver gets 8 rows from every sender.
All inputs are finite; a program needn't handle non-finite values.
Results may differ from the reference program's by a relative error of at most 0.0044.
Values may be sent and summed in bfloat16 or wider, within the bound.
No kernel may reach another device: no remote copies, remote signals or barrier semaphores. Data moves between devices by JAX's collectives and lax.ppermute only.
A program may use at most 128 MiB of HBM per device.

```python
import jax
import jax.numpy as jnp
from jax import lax

D = 768
TILE = 256
TPR = 4
NDENSE = 8
SLOT = 8
PEERS = 32
ROWS_DEV = 2048
NODES = 65536
NBLOCKS = 256


def draw_dense_ids(key, part):
    first_key = jax.random.fold_in(key, 11)
    second_key = jax.random.fold_in(key, 12)
    middle = 1 + jax.random.permutation(first_key, NBLOCKS - 2)[:NDENSE - 2]
    chosen = jnp.concatenate([jnp.array([NBLOCKS - 1, 0], dtype=jnp.int32), middle.astype(jnp.int32)])
    return chosen[jax.random.permutation(second_key, NDENSE)].astype(jnp.int32)


def draw_sparse_rows(key, part):
    rows_key = jax.random.fold_in(key, 21)
    picked = jax.random.randint(rows_key, (PEERS, PEERS, SLOT), 0, ROWS_DEV, dtype=jnp.int32)
    flat_ids = jnp.arange(PEERS * PEERS * SLOT, dtype=jnp.int32).reshape(PEERS, PEERS, SLOT)
    picked = jnp.where(flat_ids == 0, 0, picked)
    picked = jnp.where(flat_ids == SLOT, ROWS_DEV - 1, picked)
    return picked.astype(jnp.int32)


def draw_sparse_counts(key, part):
    count_key = jax.random.fold_in(key, 31)
    complete_random_key = jax.random.fold_in(key, 32)
    counts = jax.random.randint(count_key, (PEERS, PEERS), 1, SLOT + 1, dtype=jnp.int32)
    complete_target = jax.random.randint(complete_random_key, (), 0, PEERS, dtype=jnp.int32)
    column_ids = jnp.arange(PEERS, dtype=jnp.int32)[None, :]
    return jnp.where(column_ids == complete_target, SLOT, counts).astype(jnp.int32)


def set_ends(values, stream_key, smallest, high):
    dims = values.shape
    index_at = [jax.random.randint(jax.random.fold_in(stream_key, axis), (), 0, dims[axis]) for axis in range(len(dims))]
    values = values.at[tuple(index_at)].set(smallest)
    longest = dims.index(max(dims))
    index_at[longest] = (index_at[longest] + 1) % dims[longest]
    return values.at[tuple(index_at)].set(high)


def block_scale(key, extent, split, smallest, high):
    def one(axis_at, blocks):
        steps = jax.random.uniform(jax.random.fold_in(jax.random.fold_in(key, 6), axis_at), (blocks,), jnp.float32, smallest / len(split), high / len(split))
        return jnp.repeat(jnp.exp(steps), extent[axis_at] // blocks).reshape((-1,) + (1,) * (len(extent) - axis_at - 1))

    gain = one(*split[0])
    for cut in split[1:]:
        gain = gain * one(*cut)
    return gain


def gaussian(own_key, dims, scale, most, pieces=(), held_as=jnp.bfloat16):
    values = jax.random.normal(own_key, dims, jnp.float32) * scale
    if len(pieces) > 0:
        values = block_scale(own_key, dims, pieces, -0.22, 0.18) * values
    return jnp.clip(values, min=-most, max=most).astype(held_as)


def setup_inputs(seed: int = 0) -> dict:
    key_of = jax.random.split(jax.random.key(seed), 10)
    return {
        "features": gaussian(key_of[0], (NODES, D), 1.0, 6.0, ((0, 32),)),
        "dense_edge_weights": gaussian(key_of[1], (NBLOCKS, TPR, TILE, TILE), (TPR * TILE + PEERS * SLOT) ** -0.5, 0.15625, ((0, 32),)),
        "dense_cols": set_ends(jax.random.randint(key_of[2], (NBLOCKS, TPR), 0, NDENSE), jax.random.fold_in(key_of[2], 1), 0, NDENSE - 1).astype(jnp.int32),
        "dense_ids": draw_dense_ids(jax.random.fold_in(key_of[9], 71), 0),
        "sparse_w": gaussian(key_of[4], (NODES, PEERS * SLOT), (TPR * TILE + PEERS * SLOT) ** -0.5, 0.15625, ((0, 32),)),
        "sparse_rows": draw_sparse_rows(jax.random.fold_in(key_of[9], 71), 0),
        "sparse_counts": draw_sparse_counts(jax.random.fold_in(key_of[9], 71), 0),
        "weight": gaussian(key_of[7], (D, D), D ** -0.5, 0.21875),
        "bias": gaussian(key_of[8], (D,), 0.5, 3.0, (), jnp.float32),
    }


def reference(features, dense_edge_weights, dense_cols, dense_ids, sparse_w, sparse_rows, sparse_counts, weight, bias):
    blocks = features.reshape(NODES // TILE, TILE, D)
    dense_bands = blocks[dense_ids]

    def dense_block(args):
        vals, cols = args
        dense_sum = jnp.zeros((TILE, D), jnp.float32)
        for tile_index in range(TPR):
            dense_sum = dense_sum + jnp.dot(vals[tile_index], dense_bands[cols[tile_index]], preferred_element_type=jnp.float32)
        return dense_sum

    dense_part = lax.map(dense_block, (dense_edge_weights, dense_cols)).reshape(NODES, D)
    owners = features.reshape(PEERS, ROWS_DEV, D)
    slot_ids = jnp.arange(SLOT, dtype=jnp.int32)

    def sparse_dest(args):
        rows_to, counts_to, w_rows = args
        picked = jnp.take_along_axis(owners, rows_to[:, :, None].astype(jnp.int32), axis=1)
        live_slots = slot_ids[None, :] < counts_to[:, None]
        picked = jnp.where(live_slots[:, :, None], picked, jnp.zeros((), picked.dtype))
        return jnp.dot(w_rows, picked.reshape(PEERS * SLOT, D), preferred_element_type=jnp.float32)

    sparse_part = lax.map(sparse_dest, (jnp.transpose(sparse_rows, (1, 0, 2)), jnp.transpose(sparse_counts), sparse_w.reshape(PEERS, ROWS_DEV, PEERS * SLOT)))
    aggregate = (dense_part + sparse_part.reshape(NODES, D)).astype(jnp.bfloat16)
    result = jnp.dot(aggregate, weight, preferred_element_type=jnp.float32) + bias
    return jnp.maximum(result, 0.0).astype(jnp.bfloat16)
```

```python
import functools

import jax
import jax.numpy as jnp
from jax import lax
from jax.experimental import pallas as pl
from jax.experimental.pallas import tpu as pltpu
from jax.sharding import PartitionSpec as P

AXES = ("row", "grp")
PLANE = 8


def layer_kernel(meta, *refs):
    pieces = refs[:PLANE]
    rows_in, edge, sparse, weight, bias, out, bands = refs[PLANE:]
    block = pl.program_id(0)
    tiles_per = edge.shape[1]
    stripes, piece_rows, _ = pieces[0].shape
    cols_at = pl.num_programs(0) * tiles_per

    @pl.when(block == 0)
    def _():
        for i in range(PLANE):
            at = pl.multiple_of(meta[cols_at + i] * piece_rows, piece_rows)
            for j in range(stripes):
                bands[j, pl.ds(at, piece_rows), :] = pieces[i][j]

    total = jnp.dot(sparse[...], rows_in[...], preferred_element_type=jnp.float32)
    for t in range(tiles_per):
        band = bands[meta[block * tiles_per + t]]
        total += jnp.dot(edge[0, t], band, preferred_element_type=jnp.float32)
    result = jnp.dot(total.astype(jnp.bfloat16), weight[...], preferred_element_type=jnp.float32)
    out[...] = jnp.maximum(result + bias[...], 0.0).astype(out.dtype)


def layer(meta, pieces, rows_in, edge, sparse, weight, bias):
    blocks, tiles_per, tile, _ = edge.shape
    width = weight.shape[0]
    stripes = pieces[0].shape[0]
    whole = pl.BlockSpec(memory_space=pltpu.VMEM)
    return pl.pallas_call(
        layer_kernel,
        out_shape=jax.ShapeDtypeStruct((blocks * tile, width), jnp.bfloat16),
        grid_spec=pltpu.PrefetchScalarGridSpec(
            num_scalar_prefetch=1,
            grid=(blocks,),
            in_specs=[whole] * (PLANE + 1)
            + [
                pl.BlockSpec((1, tiles_per, tile, tile), lambda b, m: (b, 0, 0, 0)),
                pl.BlockSpec((tile, sparse.shape[1]), lambda b, m: (b, 0)),
                whole,
                whole,
            ],
            out_specs=pl.BlockSpec((tile, width), lambda b, m: (b, 0)),
            scratch_shapes=[pltpu.VMEM((stripes, tile, width), jnp.bfloat16)],
        ),
        compiler_params=pltpu.CompilerParams(vmem_limit_bytes=40 * 2**20),
        cost_estimate=pl.CostEstimate(
            flops=2 * blocks * tile * width * (tiles_per * tile + sparse.shape[1] + width),
            bytes_accessed=2 * (edge.size + sparse.size + 2 * blocks * tile * width),
            transcendentals=0,
        ),
    )(meta, *pieces, rows_in, edge, sparse, weight, bias)


def spread(slots, blocks, mine, at, outgoing, flat_slot, devices):
    _, tile, width = blocks.shape
    part = tile // devices
    sends = []
    for s in range(slots):
        block = lax.dynamic_index_in_dim(blocks, at[s], 0, keepdims=False)
        block = block.reshape(PLANE, devices // PLANE, part, width)
        sends.append(block.transpose(1, 0, 2, 3).reshape(devices, part, width))
    sends.append(outgoing)
    got = lax.all_to_all(jnp.concatenate(sends, axis=1), AXES, 0, 0, tiled=True)
    held = got[:, : slots * part].reshape(devices * slots, part, width)
    stripes = jnp.take(held, flat_slot(slots), axis=0, mode="clip")
    return stripes, got[:, slots * part :].reshape(-1, width)


def on_device(features, edge, cols, ids, sparse_w, sparse_rows, sparse_counts, weight, bias):
    block_count, tiles_per, tile, _ = edge.shape
    width = features.shape[1]
    stripe_count = ids.shape[0]
    devices = sparse_rows.shape[1]
    groups = devices // PLANE
    me = lax.axis_index(AXES)
    group, place = me // PLANE, me % PLANE
    blocks = features.reshape(block_count, tile, width)

    owner = ids // block_count
    earlier = jnp.arange(stripe_count)[:, None] > jnp.arange(stripe_count)[None, :]
    slot = jnp.sum(jnp.where(earlier & (owner[:, None] == owner[None, :]), 1, 0), axis=1)
    mine = owner == me
    slot_ids = jnp.arange(stripe_count)
    at = jnp.sum(
        jnp.where(mine[None, :] & (slot[None, :] == slot_ids[:, None]), ids % block_count, 0), axis=1
    )

    outgoing = features[sparse_rows[0]]
    live = jnp.arange(sparse_rows.shape[2], dtype=jnp.int32)[None, :] < sparse_counts[0][:, None]
    outgoing = jnp.where(live[:, :, None], outgoing, jnp.zeros((), outgoing.dtype))

    def scattered(slots):
        return lambda: spread(
            slots, blocks, mine, at, outgoing, lambda s: owner * s + slot, devices
        )

    held, rows_in = lax.cond(
        jnp.max(slot) < 2, scattered(2), scattered(min(stripe_count, block_count))
    )

    def swap(x, mask):
        return lax.ppermute(x, AXES, [(d, d ^ mask) for d in range(devices)])

    parts = [held] + [swap(held, PLANE * g) for g in range(1, groups)]
    ordered = [lax.select_n(group, *[parts[q ^ g] for g in range(groups)]) for q in range(groups)]
    piece = jnp.concatenate(ordered, axis=1)
    pieces = []
    for xy in range(0, PLANE, 2):
        got = swap(piece, xy) if xy else piece
        pieces += [got, swap(got, 1)]
    meta = jnp.concatenate(
        [cols.reshape(-1), place ^ jnp.arange(PLANE, dtype=jnp.int32)]
    ).astype(jnp.int32)
    return layer(meta, pieces, rows_in, edge, sparse_w, weight, bias.reshape(1, -1))


def solution(mesh):
    placed = (
        P(AXES, None),
        P(AXES, None, None, None),
        P(AXES, None),
        P(),
        P(AXES, None),
        P(AXES, None, None),
        P(AXES, None),
        P(),
        P(),
    )
    return jax.shard_map(
        on_device, mesh=mesh, in_specs=placed, out_specs=P(AXES, None), check_vma=False
    )
```

```python
import functools

import jax
import jax.numpy as jnp
from jax import lax
from jax.experimental import pallas as pl
from jax.experimental.pallas import tpu as pltpu
from jax.sharding import PartitionSpec as P

AXES = ("row", "grp")
PLANE = 8
SLOTS = 2
VMEM = pl.BlockSpec(memory_space=pltpu.VMEM)
SMEM = pl.BlockSpec(memory_space=pltpu.SMEM)
HBM = pl.BlockSpec(memory_space=pl.ANY)


def params(mib):
    return pltpu.CompilerParams(vmem_limit_bytes=mib * 2**20)


def held_in_vmem(x):
    return pltpu.with_memory_space_constraint(x, pltpu.VMEM)


def send_kernel(ids, blocks, out, sems):
    me = lax.axis_index(AXES)
    count, _, groups, _, _ = blocks.shape
    slots = out.shape[1]
    held = jnp.int32(0)
    at = [jnp.int32(0)] * slots
    for j in range(ids.shape[0]):
        own = ids[j] // count == me
        for s in range(slots):
            at[s] = jnp.where(own & (held == s), ids[j] % count, at[s])
        held = held + own.astype(jnp.int32)
    copies = []
    for s in range(slots):
        for g in range(groups):
            copies.append(
                pltpu.make_async_copy(
                    blocks.at[at[s], :, g],
                    out.at[pl.ds(g * PLANE, PLANE), s],
                    sems.at[len(copies)],
                )
            )
            copies[-1].start()
    for copy in copies:
        copy.wait()


def send_layout(slots, ids, blocks, devices):
    count, tile, width = blocks.shape
    part = tile // devices
    groups = devices // PLANE
    return pl.pallas_call(
        send_kernel,
        out_shape=jax.ShapeDtypeStruct((devices, slots, part, width), blocks.dtype),
        in_specs=[SMEM, HBM],
        out_specs=VMEM,
        scratch_shapes=[pltpu.SemaphoreType.DMA((slots * groups,))],
        compiler_params=params(16),
    )(ids, blocks.reshape(count, PLANE, groups, part, width))


def rows_kernel(rows, counts, features, weight, out):
    slots, peers = rows.shape
    n = slots * peers
    slot = lax.broadcasted_iota(jnp.int32, (slots, peers), 0)
    wanted = jnp.where(slot < counts[...], rows[...], -1).astype(jnp.float32)
    line = lax.broadcasted_iota(jnp.int32, (n, peers), 0)
    peer = lax.broadcasted_iota(jnp.int32, (n, peers), 1)
    spread = jnp.where(line // slots == peer, 1.0, 0.0)
    by_slot = lax.dot_general(
        spread, wanted, (((1,), (1,)), ((), ())), precision=lax.Precision.HIGHEST,
        preferred_element_type=jnp.float32,
    )
    line = lax.broadcasted_iota(jnp.int32, (n, slots), 0)
    slot = lax.broadcasted_iota(jnp.int32, (n, slots), 1)
    row = jnp.sum(jnp.where(line % slots == slot, by_slot, 0.0), axis=1, keepdims=True)
    row = jnp.round(row).astype(jnp.int32)
    hit = row == lax.broadcasted_iota(jnp.int32, (n, features.shape[0]), 1)
    picked = jnp.where(hit, 1.0, 0.0).astype(jnp.bfloat16)
    picked = jnp.dot(picked, features[...], preferred_element_type=jnp.float32)
    picked = jnp.dot(
        picked.astype(jnp.bfloat16), weight[...], preferred_element_type=jnp.float32
    )
    out[...] = picked.astype(out.dtype)


def listed_rows(rows, counts, features, weight):
    peers, slots = rows.shape
    return pl.pallas_call(
        rows_kernel,
        out_shape=jax.ShapeDtypeStruct((peers * slots, weight.shape[1]), features.dtype),
        in_specs=[VMEM] * 4,
        out_specs=VMEM,
        compiler_params=params(24),
    )(rows.T, counts.reshape(1, -1), features, held_in_vmem(weight))


def pick_kernel(count, ids, got, weight, out):
    n = ids.shape[0]
    owners = [ids[j] // count for j in range(n)]
    parts = []
    for j in range(n):
        slot = jnp.int32(0)
        for i in range(j):
            slot = slot + (owners[i] == owners[j]).astype(jnp.int32)
        part = got[owners[j], jnp.minimum(slot, got.shape[1] - 1)]
        parts.append(part.astype(jnp.float32))
    rows = jnp.concatenate(parts).astype(jnp.bfloat16)
    result = jnp.dot(rows, weight[...], preferred_element_type=jnp.float32)
    out[...] = result.reshape(out.shape).astype(out.dtype)


def pick(ids, got, weight, count):
    return pl.pallas_call(
        functools.partial(pick_kernel, count),
        out_shape=jax.ShapeDtypeStruct((ids.shape[0], *got.shape[2:]), got.dtype),
        in_specs=[SMEM, VMEM, VMEM],
        out_specs=VMEM,
        compiler_params=params(16),
    )(ids, got, held_in_vmem(weight))


def layer_kernel(group, meta, *refs):
    near, far = refs[:6], refs[6:10]
    rows_in, edge, sparse, bias, out, bands = refs[10:]
    first = pl.program_id(0) * group
    blocks = pl.num_programs(0) * group
    _, tiles_per, tile, _ = edge.shape
    stripes, piece_rows, width = near[0].shape
    half = width // 2

    @pl.when(first == 0)
    def _():
        for i in range(PLANE):
            at = pl.multiple_of(meta[blocks * tiles_per + i] * piece_rows, piece_rows)
            for j in range(stripes):
                if i < 6:
                    bands[j, pl.ds(at, piece_rows), :] = near[i][j]
                else:
                    bands[j, pl.ds(at, piece_rows), :half] = far[i - 6][j]
                    bands[j, pl.ds(at, piece_rows), half:] = far[i - 4][j]

    for k in range(group):
        rows = slice(k * tile, (k + 1) * tile)
        total = jnp.dot(sparse[rows], rows_in[...], preferred_element_type=jnp.float32)
        for t in range(tiles_per):
            band = bands[meta[(first + k) * tiles_per + t]]
            total += jnp.dot(edge[k, t], band, preferred_element_type=jnp.float32)
        out[rows] = jnp.maximum(total + bias[...], 0.0).astype(out.dtype)


def layer(meta, pieces, rows_in, edge, sparse, bias, group=2):
    blocks, tiles_per, tile, _ = edge.shape
    stripes, _, width = pieces[0].shape
    return pl.pallas_call(
        functools.partial(layer_kernel, group),
        out_shape=jax.ShapeDtypeStruct((blocks * tile, width), jnp.bfloat16),
        grid_spec=pltpu.PrefetchScalarGridSpec(
            num_scalar_prefetch=1,
            grid=(blocks // group,),
            in_specs=[VMEM] * (len(pieces) + 1)
            + [
                pl.BlockSpec((group, tiles_per, tile, tile), lambda b, m: (b, 0, 0, 0)),
                pl.BlockSpec((group * tile, sparse.shape[1]), lambda b, m: (b, 0)),
                VMEM,
            ],
            out_specs=pl.BlockSpec((group * tile, width), lambda b, m: (b, 0)),
            scratch_shapes=[pltpu.VMEM((stripes, tile, width), jnp.bfloat16)],
        ),
        compiler_params=params(24),
        cost_estimate=pl.CostEstimate(
            flops=2 * blocks * tile * width * (tiles_per * tile + sparse.shape[1]),
            bytes_accessed=2 * (edge.size + sparse.size + blocks * tile * width),
            transcendentals=0,
        ),
    )(
        meta,
        *[held_in_vmem(x) for x in (*pieces, rows_in)],
        pltpu.with_memory_space_constraint(edge, pltpu.HBM),
        pltpu.with_memory_space_constraint(sparse, pltpu.HBM),
        held_in_vmem(bias),
    )


def on_device(features, edge, cols, ids, sparse_w, sparse_rows, sparse_counts, weight, bias):
    block_count, tiles_per, tile, _ = edge.shape
    width = features.shape[1]
    stripe_count = ids.shape[0]
    devices = sparse_rows.shape[1]
    groups = devices // PLANE
    me = lax.axis_index(AXES)
    group, place = me // PLANE, me % PLANE
    blocks = features.reshape(block_count, tile, width)

    def exchange(x):
        return lax.all_to_all(x, AXES, 0, 0, tiled=True)

    def swap(x, mask):
        return lax.ppermute(x, AXES, [(d, d ^ mask) for d in range(devices)])

    def scattered(slots):
        return pick(ids, exchange(send_layout(slots, ids, blocks, devices)), block_count)

    sent = send_layout(SLOTS, ids, blocks, devices)
    features, sent = lax.optimization_barrier((features, sent))
    got = exchange(sent)
    outgoing = listed_rows(sparse_rows[0], sparse_counts[0], features, weight)
    got, outgoing = lax.optimization_barrier((got, outgoing))

    owner = ids // block_count
    load = jnp.max(jnp.sum((owner[:, None] == owner[None, :]).astype(jnp.int32), axis=1))
    most = min(stripe_count, block_count)
    held = lax.cond(
        load > SLOTS,
        lambda x: pick(ids, exchange(send_layout(most, ids, blocks, devices)), weight, block_count),
        lambda x: x,
        pick(ids, got, weight, block_count),
    )

    parts = [held] + [swap(held, PLANE * g) for g in range(1, groups)]
    ordered = [lax.select_n(group, *[parts[q ^ g] for g in range(groups)]) for q in range(groups)]
    own = jnp.concatenate(ordered, axis=1)

    own, outgoing = lax.optimization_barrier((own, outgoing))
    x, y = swap(own, 4), swap(own, 2)
    half = width // 2
    rows_in = exchange(outgoing.reshape(devices, -1, width)).reshape(-1, width)
    left, right = swap(x[:, :, :half], 2), swap(y[:, :, half:], 4)
    pieces = [own, swap(own, 1), y, swap(y, 1), x, swap(x, 1)]
    pieces += [left, swap(left, 1), right, swap(right, 1)]

    meta = jnp.concatenate(
        [cols.reshape(-1), place ^ jnp.arange(PLANE, dtype=jnp.int32)]
    ).astype(jnp.int32)
    return layer(meta, pieces, rows_in, edge, sparse_w, bias.reshape(1, -1))


def solution(mesh):
    placed = (
        P(AXES, None),
        P(AXES, None, None, None),
        P(AXES, None),
        P(),
        P(AXES, None),
        P(AXES, None, None),
        P(AXES, None),
        P(),
        P(),
    )
    return jax.shard_map(
        on_device, mesh=mesh, in_specs=placed, out_specs=P(AXES, None), check_vma=False
    )
```

```python
import functools

import jax
import jax.numpy as jnp
from jax import lax
from jax.experimental import pallas as pl
from jax.experimental.pallas import tpu as pltpu
from jax.sharding import PartitionSpec as P

AXES = ("row", "grp")
PLANE = 8
SLOTS = 3
PLANE_SLOTS = 5
VMEM = pl.BlockSpec(memory_space=pltpu.VMEM)
SMEM = pl.BlockSpec(memory_space=pltpu.SMEM)
HBM = pl.BlockSpec(memory_space=pl.ANY)


def params(mib):
    return pltpu.CompilerParams(vmem_limit_bytes=mib * 2**20)


def held_in_vmem(x):
    return pltpu.with_memory_space_constraint(x, pltpu.VMEM)


def scan(ids, mine, fields):
    held = jnp.int32(0)
    found = [[jnp.int32(0)] * SLOTS for _ in fields]
    for j in range(ids.shape[0]):
        own = mine(ids[j])
        for f, field in enumerate(fields):
            for s in range(SLOTS):
                found[f][s] = jnp.where(own & (held == s), field(ids[j]), found[f][s])
        held = held + own.astype(jnp.int32)
    return found


def slot_of(ids, j, unit):
    slot = jnp.int32(0)
    for i in range(j):
        slot = slot + (ids[i] // unit == ids[j] // unit).astype(jnp.int32)
    return slot


def halves_kernel(ids, blocks, keep, give, sems):
    me = lax.axis_index(AXES)
    count = blocks.shape[0]
    core = me % 2
    (at,) = scan(ids, lambda i: i // (2 * count) == me // 2, [lambda i: i % count])
    copies = []
    for s in range(SLOTS):
        for out, half in ((give, 1 - core), (keep, core)):
            copies.append(
                pltpu.make_async_copy(blocks.at[at[s], :, half], out.at[:, s], sems.at[len(copies)])
            )
            copies[-1].start()
    for copy in copies:
        copy.wait()


def halves(ids, blocks, devices):
    count, tile, width = blocks.shape
    part = tile // devices
    groups = devices // PLANE
    shape = pltpu.VMEM((PLANE // 2, SLOTS, groups, part, width), blocks.dtype)
    return pl.pallas_call(
        halves_kernel,
        out_shape=[shape, shape],
        in_specs=[SMEM, HBM],
        out_specs=[VMEM, VMEM],
        scratch_shapes=[pltpu.SemaphoreType.DMA((2 * SLOTS,))],
        compiler_params=params(16),
    )(ids, blocks.reshape(count, PLANE // 2, 2, groups, part, width))


def merge_kernel(count, ids, keep, got, *outs):
    me = lax.axis_index(AXES)
    core, place = me % 2, me % PLANE // 2
    (cores,) = scan(
        ids, lambda i: i // (2 * count) == me // 2, [lambda i: i // count % 2]
    )
    for s in range(SLOTS):

        @pl.when(cores[s] == core)
        def _():
            for m, out in enumerate(outs):
                out[s] = keep[place ^ m, s]

        @pl.when(cores[s] != core)
        def _():
            for m, out in enumerate(outs):
                out[s] = got[place ^ m, s]


def merge(ids, keep, got, count):
    shape = pltpu.VMEM(keep.shape[1:], keep.dtype)
    return pl.pallas_call(
        functools.partial(merge_kernel, count),
        out_shape=[shape] * keep.shape[0],
        in_specs=[SMEM, VMEM, VMEM],
        out_specs=[VMEM] * keep.shape[0],
        compiler_params=params(16),
    )(ids, held_in_vmem(keep), held_in_vmem(got))


def sort_kernel(count, ids, *refs):
    near, outs = refs[: PLANE // 2], refs[PLANE // 2 :]
    me = lax.axis_index(AXES)
    group, place = me // PLANE, me % PLANE // 2
    for j in range(ids.shape[0]):
        owner = ids[j] // count
        slot = jnp.minimum(slot_of(ids, j, 2 * count), SLOTS - 1)
        to = jnp.minimum(slot_of(ids, j, PLANE * count), PLANE_SLOTS - 1)
        for m, ref in enumerate(near):

            @pl.when((owner // PLANE == group) & (owner % PLANE // 2 ^ place == m))
            def _():
                for g, out in enumerate(outs):
                    out[to] = ref[slot, group ^ g]


def sort(ids, near, count):
    _, groups, part, width = near[0].shape
    shape = pltpu.VMEM((PLANE_SLOTS, part, width), near[0].dtype)
    return pl.pallas_call(
        functools.partial(sort_kernel, count),
        out_shape=[shape] * groups,
        in_specs=[SMEM] + [VMEM] * len(near),
        out_specs=[VMEM] * groups,
        compiler_params=params(16),
    )(ids, *[held_in_vmem(x) for x in near])


def choose_kernel(count, ids, *refs):
    arrived, weight, out = refs[:-2], refs[-2], refs[-1]
    group = lax.axis_index(AXES) // PLANE
    parts = []
    for j in range(ids.shape[0]):
        at = group ^ ids[j] // (count * PLANE)
        slot = jnp.minimum(slot_of(ids, j, PLANE * count), PLANE_SLOTS - 1)
        part = arrived[0][slot].astype(jnp.float32)
        for g in range(1, len(arrived)):
            part = jnp.where(at == g, arrived[g][slot].astype(jnp.float32), part)
        parts.append(part)
    rows = jnp.concatenate(parts).astype(jnp.bfloat16)
    result = jnp.dot(rows, weight[...], preferred_element_type=jnp.float32)
    out[...] = result.reshape(out.shape).astype(out.dtype)


def choose(ids, arrived, weight, count):
    return pl.pallas_call(
        functools.partial(choose_kernel, count),
        out_shape=jax.ShapeDtypeStruct((ids.shape[0], *arrived[0].shape[1:]), arrived[0].dtype),
        in_specs=[SMEM] + [VMEM] * (len(arrived) + 1),
        out_specs=VMEM,
        compiler_params=params(16),
    )(ids, *[held_in_vmem(x) for x in arrived], held_in_vmem(weight))


def send_kernel(ids, blocks, out, sems):
    me = lax.axis_index(AXES)
    count, _, groups, _, _ = blocks.shape
    slots = out.shape[1]
    held = jnp.int32(0)
    at = [jnp.int32(0)] * slots
    for j in range(ids.shape[0]):
        own = ids[j] // count == me
        for s in range(slots):
            at[s] = jnp.where(own & (held == s), ids[j] % count, at[s])
        held = held + own.astype(jnp.int32)
    copies = []
    for s in range(slots):
        for g in range(groups):
            copies.append(
                pltpu.make_async_copy(
                    blocks.at[at[s], :, g],
                    out.at[pl.ds(g * PLANE, PLANE), s],
                    sems.at[len(copies)],
                )
            )
            copies[-1].start()
    for copy in copies:
        copy.wait()


def send_layout(slots, ids, blocks, devices):
    count, tile, width = blocks.shape
    part = tile // devices
    groups = devices // PLANE
    return pl.pallas_call(
        send_kernel,
        out_shape=jax.ShapeDtypeStruct((devices, slots, part, width), blocks.dtype),
        in_specs=[SMEM, HBM],
        out_specs=VMEM,
        scratch_shapes=[pltpu.SemaphoreType.DMA((slots * groups,))],
        compiler_params=params(16),
    )(ids, blocks.reshape(count, PLANE, groups, part, width))


def rows_kernel(rows, counts, features, weight, *outs):
    slots, peers = rows.shape
    n = slots * peers
    groups = peers // PLANE
    me = lax.axis_index(AXES)
    slot = lax.broadcasted_iota(jnp.int32, (slots, peers), 0)
    wanted = jnp.where(slot < counts[...], rows[...], -1).astype(jnp.float32)
    at = lax.broadcasted_iota(jnp.int32, (n, peers), 0) // slots
    away = at % groups * PLANE + at // groups % (PLANE // 2) * 2 + at // (groups * PLANE // 2)
    peer = lax.broadcasted_iota(jnp.int32, (n, peers), 1)
    spread = jnp.where(away ^ peer == me, 1.0, 0.0)
    by_slot = lax.dot_general(
        spread, wanted, (((1,), (1,)), ((), ())), precision=lax.Precision.HIGHEST,
        preferred_element_type=jnp.float32,
    )
    line = lax.broadcasted_iota(jnp.int32, (n, slots), 0)
    slot = lax.broadcasted_iota(jnp.int32, (n, slots), 1)
    row = jnp.sum(jnp.where(line % slots == slot, by_slot, 0.0), axis=1, keepdims=True)
    row = jnp.round(row).astype(jnp.int32)
    hit = row == lax.broadcasted_iota(jnp.int32, (n, features.shape[0]), 1)
    picked = jnp.where(hit, 1.0, 0.0).astype(jnp.bfloat16)
    picked = jnp.dot(picked, features[...], preferred_element_type=jnp.float32)
    picked = jnp.dot(
        picked.astype(jnp.bfloat16), weight[...], preferred_element_type=jnp.float32
    )
    picked = picked.reshape(len(outs), *outs[0].shape)
    for core, out in enumerate(outs):
        out[...] = picked[core].astype(out.dtype)


def listed_rows(rows, counts, features, weight):
    peers, slots = rows.shape
    shape = pltpu.VMEM((PLANE // 2, peers // PLANE, slots, weight.shape[1]), features.dtype)
    return pl.pallas_call(
        rows_kernel,
        out_shape=[shape, shape],
        in_specs=[VMEM] * 4,
        out_specs=[VMEM] * 2,
        compiler_params=params(24),
    )(rows.T, counts.reshape(1, -1), features, held_in_vmem(weight))


def pick_kernel(count, ids, got, weight, out):
    n = ids.shape[0]
    parts = []
    for j in range(n):
        slot = jnp.minimum(slot_of(ids, j, count), got.shape[1] - 1)
        parts.append(got[ids[j] // count, slot].astype(jnp.float32))
    rows = jnp.concatenate(parts).astype(jnp.bfloat16)
    result = jnp.dot(rows, weight[...], preferred_element_type=jnp.float32)
    out[...] = result.reshape(out.shape).astype(out.dtype)


def pick(ids, got, weight, count):
    return pl.pallas_call(
        functools.partial(pick_kernel, count),
        out_shape=jax.ShapeDtypeStruct((ids.shape[0], *got.shape[2:]), got.dtype),
        in_specs=[SMEM, VMEM, VMEM],
        out_specs=VMEM,
        compiler_params=params(16),
    )(ids, got, held_in_vmem(weight))


def layer_kernel(group, meta, *refs):
    near, far = refs[:6], refs[6:10]
    listed, refs = refs[10:-7], refs[-7:]
    edge, sparse, bias, out, bands, rows_f32, rows_in = refs
    first = pl.program_id(0) * group
    blocks = pl.num_programs(0) * group
    _, tiles_per, tile, _ = edge.shape
    stripes, piece_rows, width = near[0].shape
    half = width // 2

    @pl.when(first == 0)
    def _():
        for i in range(PLANE):
            at = pl.multiple_of(meta[blocks * tiles_per + i] * piece_rows, piece_rows)
            for j in range(stripes):
                if i < 6:
                    bands[j, pl.ds(at, piece_rows), :] = near[i][j]
                else:
                    bands[j, pl.ds(at, piece_rows), :half] = far[i - 6][j]
                    bands[j, pl.ds(at, piece_rows), half:] = far[i - 4][j]
        me = lax.axis_index(AXES)
        slots = listed[0].shape[2]
        for g, ref in enumerate(listed):
            for m in range(PLANE // 2):
                for k in range(2):
                    at = pl.multiple_of((me ^ (g * PLANE + m * 2 + k)) * slots, slots)
                    rows_f32[pl.ds(at, slots), :] = ref[m, k].astype(jnp.float32)
        rows_in[...] = rows_f32[...].astype(rows_in.dtype)

    for k in range(group):
        rows = slice(k * tile, (k + 1) * tile)
        total = jnp.dot(sparse[rows], rows_in[...], preferred_element_type=jnp.float32)
        for t in range(tiles_per):
            band = bands[meta[(first + k) * tiles_per + t]]
            total += jnp.dot(edge[k, t], band, preferred_element_type=jnp.float32)
        out[rows] = jnp.maximum(total + bias[...], 0.0).astype(out.dtype)


def layer(meta, pieces, listed, edge, sparse, bias, group=2):
    blocks, tiles_per, tile, _ = edge.shape
    stripes, _, width = pieces[0].shape
    lines = sparse.shape[1]
    return pl.pallas_call(
        functools.partial(layer_kernel, group),
        out_shape=jax.ShapeDtypeStruct((blocks * tile, width), jnp.bfloat16),
        grid_spec=pltpu.PrefetchScalarGridSpec(
            num_scalar_prefetch=1,
            grid=(blocks // group,),
            in_specs=[VMEM] * (len(pieces) + len(listed))
            + [
                pl.BlockSpec((group, tiles_per, tile, tile), lambda b, m: (b, 0, 0, 0)),
                pl.BlockSpec((group * tile, lines), lambda b, m: (b, 0)),
                VMEM,
            ],
            out_specs=pl.BlockSpec((group * tile, width), lambda b, m: (b, 0)),
            scratch_shapes=[
                pltpu.VMEM((stripes, tile, width), jnp.bfloat16),
                pltpu.VMEM((lines, width), jnp.float32),
                pltpu.VMEM((lines, width), jnp.bfloat16),
            ],
        ),
        compiler_params=params(24),
        cost_estimate=pl.CostEstimate(
            flops=2 * blocks * tile * width * (tiles_per * tile + lines),
            bytes_accessed=2 * (edge.size + sparse.size + blocks * tile * width),
            transcendentals=0,
        ),
    )(
        meta,
        *[held_in_vmem(x) for x in (*pieces, *listed)],
        pltpu.with_memory_space_constraint(edge, pltpu.HBM),
        pltpu.with_memory_space_constraint(sparse, pltpu.HBM),
        held_in_vmem(bias),
    )


def on_device(features, edge, cols, ids, sparse_w, sparse_rows, sparse_counts, weight, bias):
    block_count, tiles_per, tile, _ = edge.shape
    width = features.shape[1]
    stripe_count = ids.shape[0]
    devices = sparse_rows.shape[1]
    groups = devices // PLANE
    me = lax.axis_index(AXES)
    group, place = me // PLANE, me % PLANE
    blocks = features.reshape(block_count, tile, width)

    def exchange(x):
        return lax.all_to_all(x, AXES, 0, 0, tiled=True)

    def swap(x, mask):
        return lax.ppermute(x, AXES, [(d, d ^ mask) for d in range(devices)])

    def scattered(slots):
        return pick(ids, exchange(send_layout(slots, ids, blocks, devices)), block_count)

    keep, give = halves(ids, blocks, devices)
    sent = merge(ids, keep, swap(give, 1), block_count)
    near = [sent[0]] + [swap(x, 2 * m) for m, x in enumerate(sent) if m > 0]

    features, _ = lax.optimization_barrier((features, sent[0]))
    for_own, for_pair = listed_rows(sparse_rows[0], sparse_counts[0], features, weight)
    near[1], for_pair = lax.optimization_barrier((near[1], for_pair))
    from_pair = swap(for_pair, 1)

    over = sort(ids, near, block_count)
    arrived = [over[0]] + [swap(x, PLANE * g) for g, x in enumerate(over) if g > 0]

    from_pair, _ = lax.optimization_barrier((from_pair, over[0]))
    listed = [jnp.stack([for_own[m], from_pair[m]]) for m in range(PLANE // 2)]
    listed = [swap(x, 2 * m) if m else x for m, x in enumerate(listed)]

    arrived[1], *listed = lax.optimization_barrier((arrived[1], *listed))

    def load(unit):
        at = ids // unit
        return jnp.max(jnp.sum((at[:, None] == at[None, :]).astype(jnp.int32), axis=1))

    full = (load(2 * block_count) > SLOTS) | (load(PLANE * block_count) > PLANE_SLOTS)
    most = min(stripe_count, block_count)
    held = lax.cond(
        full,
        lambda x: pick(ids, exchange(send_layout(most, ids, blocks, devices)), weight, block_count),
        lambda x: x,
        choose(ids, arrived, weight, block_count),
    )

    parts = [held] + [swap(held, PLANE * g) for g in range(1, groups)]
    ordered = [lax.select_n(group, *[parts[q ^ g] for g in range(groups)]) for q in range(groups)]
    own = jnp.concatenate(ordered, axis=1)

    own, *listed = lax.optimization_barrier((own, *listed))
    x, y = swap(own, 4), swap(own, 2)
    listed = [jnp.stack([r[:, g] for r in listed]) for g in range(groups)]
    listed = [swap(r, PLANE * g) if g else r for g, r in enumerate(listed)]
    half = width // 2
    left, right = swap(x[:, :, :half], 2), swap(y[:, :, half:], 4)
    pieces = [own, swap(own, 1), y, swap(y, 1), x, swap(x, 1)]
    pieces += [left, swap(left, 1), right, swap(right, 1)]

    meta = jnp.concatenate(
        [cols.reshape(-1), place ^ jnp.arange(PLANE, dtype=jnp.int32)]
    ).astype(jnp.int32)
    return layer(meta, pieces, listed, edge, sparse_w, bias.reshape(1, -1))


def solution(mesh):
    placed = (
        P(AXES, None),
        P(AXES, None, None, None),
        P(AXES, None),
        P(),
        P(AXES, None),
        P(AXES, None, None),
        P(AXES, None),
        P(),
        P(),
    )
    return jax.shard_map(
        on_device, mesh=mesh, in_specs=placed, out_specs=P(AXES, None), check_vma=False
    )
```

```python
import functools

import jax
import jax.numpy as jnp
from jax import lax
from jax.experimental import pallas as pl
from jax.experimental.pallas import tpu as pltpu
from jax.sharding import PartitionSpec as P

AXES = ("row", "grp")
PLANE = 8
SLOTS = 3
PLANE_SLOTS = 5
VMEM = pl.BlockSpec(memory_space=pltpu.VMEM)
SMEM = pl.BlockSpec(memory_space=pltpu.SMEM)
HBM = pl.BlockSpec(memory_space=pl.ANY)


def params(mib):
    return pltpu.CompilerParams(vmem_limit_bytes=mib * 2**20)


def held_in_vmem(x):
    return pltpu.with_memory_space_constraint(x, pltpu.VMEM)


def scan(ids, mine, fields):
    held = jnp.int32(0)
    found = [[jnp.int32(0)] * SLOTS for _ in fields]
    for j in range(ids.shape[0]):
        own = mine(ids[j])
        for f, field in enumerate(fields):
            for s in range(SLOTS):
                found[f][s] = jnp.where(own & (held == s), field(ids[j]), found[f][s])
        held = held + own.astype(jnp.int32)
    return found


def slot_of(ids, j, unit):
    slot = jnp.int32(0)
    for i in range(j):
        slot = slot + (ids[i] // unit == ids[j] // unit).astype(jnp.int32)
    return slot


def halves_kernel(ids, blocks, keep, give, sems):
    me = lax.axis_index(AXES)
    count = blocks.shape[0]
    core = me % 2
    (at,) = scan(ids, lambda i: i // (2 * count) == me // 2, [lambda i: i % count])
    copies = []
    for s in range(SLOTS):
        for out, half in ((give, 1 - core), (keep, core)):
            copies.append(
                pltpu.make_async_copy(blocks.at[at[s], :, half], out.at[:, s], sems.at[len(copies)])
            )
            copies[-1].start()
    for copy in copies:
        copy.wait()


def halves(ids, blocks, devices):
    count, tile, width = blocks.shape
    part = tile // devices
    groups = devices // PLANE
    shape = pltpu.VMEM((PLANE // 2, SLOTS, groups, part, width), blocks.dtype)
    return pl.pallas_call(
        halves_kernel,
        out_shape=[shape, shape],
        in_specs=[SMEM, HBM],
        out_specs=[VMEM, VMEM],
        scratch_shapes=[pltpu.SemaphoreType.DMA((2 * SLOTS,))],
        compiler_params=params(16),
    )(ids, blocks.reshape(count, PLANE // 2, 2, groups, part, width))


def merge_kernel(count, ids, keep, got, *outs):
    me = lax.axis_index(AXES)
    core, place = me % 2, me % PLANE // 2
    (cores,) = scan(
        ids, lambda i: i // (2 * count) == me // 2, [lambda i: i // count % 2]
    )
    for s in range(SLOTS):

        @pl.when(cores[s] == core)
        def _():
            for m, out in enumerate(outs):
                out[s] = keep[place ^ m, s]

        @pl.when(cores[s] != core)
        def _():
            for m, out in enumerate(outs):
                out[s] = got[place ^ m, s]


def merge(ids, keep, got, count):
    shape = pltpu.VMEM(keep.shape[1:], keep.dtype)
    return pl.pallas_call(
        functools.partial(merge_kernel, count),
        out_shape=[shape] * keep.shape[0],
        in_specs=[SMEM, VMEM, VMEM],
        out_specs=[VMEM] * keep.shape[0],
        compiler_params=params(16),
    )(ids, held_in_vmem(keep), held_in_vmem(got))


def sort_kernel(count, ids, *refs):
    near, outs = refs[: PLANE // 2], refs[PLANE // 2 :]
    me = lax.axis_index(AXES)
    group, place = me // PLANE, me % PLANE // 2
    for j in range(ids.shape[0]):
        owner = ids[j] // count
        slot = jnp.minimum(slot_of(ids, j, 2 * count), SLOTS - 1)
        to = jnp.minimum(slot_of(ids, j, PLANE * count), PLANE_SLOTS - 1)
        for m, ref in enumerate(near):

            @pl.when((owner // PLANE == group) & (owner % PLANE // 2 ^ place == m))
            def _():
                for g, out in enumerate(outs):
                    out[to] = ref[slot, group ^ g]


def sort(ids, near, count):
    _, groups, part, width = near[0].shape
    shape = pltpu.VMEM((PLANE_SLOTS, part, width), near[0].dtype)
    return pl.pallas_call(
        functools.partial(sort_kernel, count),
        out_shape=[shape] * groups,
        in_specs=[SMEM] + [VMEM] * len(near),
        out_specs=[VMEM] * groups,
        compiler_params=params(16),
    )(ids, *[held_in_vmem(x) for x in near])


def choose_kernel(count, ids, full, *refs):
    arrived, (spare, weight, out) = refs[:-3], refs[-3:]
    group = lax.axis_index(AXES) // PLANE
    parts = []
    for j in range(ids.shape[0]):
        at = group ^ ids[j] // (count * PLANE)
        slot = jnp.minimum(slot_of(ids, j, PLANE * count), PLANE_SLOTS - 1)
        part = arrived[0][slot].astype(jnp.float32)
        for g in range(1, len(arrived)):
            part = jnp.where(at == g, arrived[g][slot].astype(jnp.float32), part)
        parts.append(part)
    rows = jnp.concatenate(parts).astype(jnp.bfloat16)
    result = jnp.dot(rows, weight[...], preferred_element_type=jnp.float32)
    result = result.reshape(out.shape)
    out[...] = jnp.where(full[0] > 0, spare[...].astype(jnp.float32), result).astype(out.dtype)


def choose(ids, full, arrived, spare, weight, count):
    return pl.pallas_call(
        functools.partial(choose_kernel, count),
        out_shape=jax.ShapeDtypeStruct((ids.shape[0], *arrived[0].shape[1:]), arrived[0].dtype),
        in_specs=[SMEM, SMEM] + [VMEM] * (len(arrived) + 2),
        out_specs=VMEM,
        compiler_params=params(16),
    )(ids, full, *[held_in_vmem(x) for x in (*arrived, spare, weight)])


def send_kernel(ids, blocks, out, sems):
    me = lax.axis_index(AXES)
    count, _, groups, _, _ = blocks.shape
    slots = out.shape[1]
    held = jnp.int32(0)
    at = [jnp.int32(0)] * slots
    for j in range(ids.shape[0]):
        own = ids[j] // count == me
        for s in range(slots):
            at[s] = jnp.where(own & (held == s), ids[j] % count, at[s])
        held = held + own.astype(jnp.int32)
    copies = []
    for s in range(slots):
        for g in range(groups):
            copies.append(
                pltpu.make_async_copy(
                    blocks.at[at[s], :, g],
                    out.at[pl.ds(g * PLANE, PLANE), s],
                    sems.at[len(copies)],
                )
            )
            copies[-1].start()
    for copy in copies:
        copy.wait()


def send_layout(slots, ids, blocks, devices):
    count, tile, width = blocks.shape
    part = tile // devices
    groups = devices // PLANE
    return pl.pallas_call(
        send_kernel,
        out_shape=jax.ShapeDtypeStruct((devices, slots, part, width), blocks.dtype),
        in_specs=[SMEM, HBM],
        out_specs=VMEM,
        scratch_shapes=[pltpu.SemaphoreType.DMA((slots * groups,))],
        compiler_params=params(16),
    )(ids, blocks.reshape(count, PLANE, groups, part, width))


def rows_kernel(rows, counts, features, weight, *outs):
    slots, peers = rows.shape
    n = slots * peers
    groups = peers // PLANE
    me = lax.axis_index(AXES)
    slot = lax.broadcasted_iota(jnp.int32, (slots, peers), 0)
    wanted = jnp.where(slot < counts[...], rows[...], -1).astype(jnp.float32)
    at = lax.broadcasted_iota(jnp.int32, (n, peers), 0) // slots
    away = at % groups * PLANE + at // groups % (PLANE // 2) * 2 + at // (groups * PLANE // 2)
    peer = lax.broadcasted_iota(jnp.int32, (n, peers), 1)
    spread = jnp.where(away ^ peer == me, 1.0, 0.0)
    by_slot = lax.dot_general(
        spread, wanted, (((1,), (1,)), ((), ())), precision=lax.Precision.HIGHEST,
        preferred_element_type=jnp.float32,
    )
    line = lax.broadcasted_iota(jnp.int32, (n, slots), 0)
    slot = lax.broadcasted_iota(jnp.int32, (n, slots), 1)
    row = jnp.sum(jnp.where(line % slots == slot, by_slot, 0.0), axis=1, keepdims=True)
    row = jnp.round(row).astype(jnp.int32)
    hit = row == lax.broadcasted_iota(jnp.int32, (n, features.shape[0]), 1)
    picked = jnp.where(hit, 1.0, 0.0).astype(jnp.bfloat16)
    picked = jnp.dot(picked, features[...], preferred_element_type=jnp.float32)
    picked = jnp.dot(
        picked.astype(jnp.bfloat16), weight[...], preferred_element_type=jnp.float32
    )
    picked = picked.reshape(len(outs), *outs[0].shape)
    for core, out in enumerate(outs):
        out[...] = picked[core].astype(out.dtype)


def listed_rows(rows, counts, features, weight):
    peers, slots = rows.shape
    shape = pltpu.VMEM((PLANE // 2, peers // PLANE, slots, weight.shape[1]), features.dtype)
    return pl.pallas_call(
        rows_kernel,
        out_shape=[shape, shape],
        in_specs=[VMEM] * 4,
        out_specs=[VMEM] * 2,
        compiler_params=params(24),
    )(rows.T, counts.reshape(1, -1), features, held_in_vmem(weight))


def pick_kernel(count, ids, got, weight, out):
    n = ids.shape[0]
    parts = []
    for j in range(n):
        slot = jnp.minimum(slot_of(ids, j, count), got.shape[1] - 1)
        parts.append(got[ids[j] // count, slot].astype(jnp.float32))
    rows = jnp.concatenate(parts).astype(jnp.bfloat16)
    result = jnp.dot(rows, weight[...], preferred_element_type=jnp.float32)
    out[...] = result.reshape(out.shape).astype(out.dtype)


def pick(ids, got, weight, count):
    return pl.pallas_call(
        functools.partial(pick_kernel, count),
        out_shape=jax.ShapeDtypeStruct((ids.shape[0], *got.shape[2:]), got.dtype),
        in_specs=[SMEM, VMEM, VMEM],
        out_specs=VMEM,
        compiler_params=params(16),
    )(ids, got, held_in_vmem(weight))


def layer_kernel(group, meta, *refs):
    near, far = refs[:6], refs[6:10]
    listed, refs = refs[10:-7], refs[-7:]
    edge, sparse, bias, out, bands, rows_f32, rows_in = refs
    first = pl.program_id(0) * group
    blocks = pl.num_programs(0) * group
    _, tiles_per, tile, _ = edge.shape
    stripes, piece_rows, width = near[0].shape
    half = width // 2

    @pl.when(first == 0)
    def _():
        for i in range(PLANE):
            at = pl.multiple_of(meta[blocks * tiles_per + i] * piece_rows, piece_rows)
            for j in range(stripes):
                if i < 6:
                    bands[j, pl.ds(at, piece_rows), :] = near[i][j]
                else:
                    bands[j, pl.ds(at, piece_rows), :half] = far[i - 6][j]
                    bands[j, pl.ds(at, piece_rows), half:] = far[i - 4][j]
        me = lax.axis_index(AXES)
        slots = listed[0].shape[2]
        for g, ref in enumerate(listed):
            for m in range(PLANE // 2):
                for k in range(2):
                    at = pl.multiple_of((me ^ (g * PLANE + m * 2 + k)) * slots, slots)
                    rows_f32[pl.ds(at, slots), :] = ref[m, k].astype(jnp.float32)
        rows_in[...] = rows_f32[...].astype(rows_in.dtype)

    for k in range(group):
        rows = slice(k * tile, (k + 1) * tile)
        total = jnp.dot(sparse[rows], rows_in[...], preferred_element_type=jnp.float32)
        for t in range(tiles_per):
            band = bands[meta[(first + k) * tiles_per + t]]
            total += jnp.dot(edge[k, t], band, preferred_element_type=jnp.float32)
        out[rows] = jnp.maximum(total + bias[...], 0.0).astype(out.dtype)


def layer(meta, pieces, listed, edge, sparse, bias, group=2):
    blocks, tiles_per, tile, _ = edge.shape
    stripes, _, width = pieces[0].shape
    lines = sparse.shape[1]
    return pl.pallas_call(
        functools.partial(layer_kernel, group),
        out_shape=jax.ShapeDtypeStruct((blocks * tile, width), jnp.bfloat16),
        grid_spec=pltpu.PrefetchScalarGridSpec(
            num_scalar_prefetch=1,
            grid=(blocks // group,),
            in_specs=[VMEM] * (len(pieces) + len(listed))
            + [
                pl.BlockSpec((group, tiles_per, tile, tile), lambda b, m: (b, 0, 0, 0)),
                pl.BlockSpec((group * tile, lines), lambda b, m: (b, 0)),
                VMEM,
            ],
            out_specs=pl.BlockSpec((group * tile, width), lambda b, m: (b, 0)),
            scratch_shapes=[
                pltpu.VMEM((stripes, tile, width), jnp.bfloat16),
                pltpu.VMEM((lines, width), jnp.float32),
                pltpu.VMEM((lines, width), jnp.bfloat16),
            ],
        ),
        compiler_params=params(24),
        cost_estimate=pl.CostEstimate(
            flops=2 * blocks * tile * width * (tiles_per * tile + lines),
            bytes_accessed=2 * (edge.size + sparse.size + blocks * tile * width),
            transcendentals=0,
        ),
    )(
        meta,
        *[held_in_vmem(x) for x in (*pieces, *listed)],
        pltpu.with_memory_space_constraint(edge, pltpu.HBM),
        pltpu.with_memory_space_constraint(sparse, pltpu.HBM),
        held_in_vmem(bias),
    )


def on_device(features, edge, cols, ids, sparse_w, sparse_rows, sparse_counts, weight, bias):
    block_count, tiles_per, tile, _ = edge.shape
    width = features.shape[1]
    stripe_count = ids.shape[0]
    devices = sparse_rows.shape[1]
    groups = devices // PLANE
    me = lax.axis_index(AXES)
    group, place = me // PLANE, me % PLANE
    blocks = features.reshape(block_count, tile, width)

    def exchange(x):
        return lax.all_to_all(x, AXES, 0, 0, tiled=True)

    def swap(x, mask):
        return lax.ppermute(x, AXES, [(d, d ^ mask) for d in range(devices)])

    def scattered(slots):
        return pick(ids, exchange(send_layout(slots, ids, blocks, devices)), block_count)

    def load(unit):
        at = ids // unit
        return jnp.max(jnp.sum((at[:, None] == at[None, :]).astype(jnp.int32), axis=1))

    full = (load(2 * block_count) > SLOTS) | (load(PLANE * block_count) > PLANE_SLOTS)
    most = min(stripe_count, block_count)
    spare = lax.cond(
        full,
        lambda: pick(ids, exchange(send_layout(most, ids, blocks, devices)), weight, block_count),
        lambda: jnp.zeros((stripe_count, tile // devices, width), features.dtype),
    )
    full = full.astype(jnp.int32)[None]

    keep, give = halves(ids, blocks, devices)
    sent = merge(ids, keep, swap(give, 1), block_count)
    near = [sent[0]] + [swap(x, 2 * m) for m, x in enumerate(sent) if m > 0]

    features, _ = lax.optimization_barrier((features, sent[0]))
    for_own, for_pair = listed_rows(sparse_rows[0], sparse_counts[0], features, weight)
    near[1], for_pair = lax.optimization_barrier((near[1], for_pair))
    from_pair = swap(for_pair, 1)

    near[2], spare = lax.optimization_barrier((near[2], spare))
    over = sort(ids, near, block_count)
    arrived = [over[0]] + [swap(x, PLANE * g) for g, x in enumerate(over) if g > 0]

    from_pair, _ = lax.optimization_barrier((from_pair, over[0]))
    both = jnp.stack([for_own, from_pair]).reshape(2, 2, 2, *for_own.shape[1:])
    across = swap(both[:, 1], 4)

    arrived[1], across = lax.optimization_barrier((arrived[1], across))

    held = choose(ids, full, arrived, spare, weight, block_count)

    parts = [held] + [swap(held, PLANE * g) for g in range(1, groups)]
    across, _ = lax.optimization_barrier((across, held))
    turned = swap(jnp.stack([both[:, 0, 1], across[:, 1]]), 2)
    listed = [both[:, 0, 0], turned[0], across[:, 0], turned[1]]
    ordered = [lax.select_n(group, *[parts[q ^ g] for g in range(groups)]) for q in range(groups)]
    own = jnp.concatenate(ordered, axis=1)

    own, *listed = lax.optimization_barrier((own, *listed))
    x, y = swap(own, 4), swap(own, 2)
    listed = [jnp.stack([r[:, g] for r in listed]) for g in range(groups)]
    listed = [swap(r, PLANE * g) if g else r for g, r in enumerate(listed)]
    half = width // 2
    left, right = swap(x[:, :, :half], 2), swap(y[:, :, half:], 4)
    pieces = [own, swap(own, 1), y, swap(y, 1), x, swap(x, 1)]
    pieces += [left, swap(left, 1), right, swap(right, 1)]

    meta = jnp.concatenate(
        [cols.reshape(-1), place ^ jnp.arange(PLANE, dtype=jnp.int32)]
    ).astype(jnp.int32)
    return layer(meta, pieces, listed, edge, sparse_w, bias.reshape(1, -1))


def solution(mesh):
    placed = (
        P(AXES, None),
        P(AXES, None, None, None),
        P(AXES, None),
        P(),
        P(AXES, None),
        P(AXES, None, None),
        P(AXES, None),
        P(),
        P(),
    )
    return jax.shard_map(
        on_device, mesh=mesh, in_specs=placed, out_specs=P(AXES, None), check_vma=False
    )
```

```python
import functools

import jax
import jax.numpy as jnp
from jax import lax
from jax.experimental import pallas as pl
from jax.experimental.pallas import tpu as pltpu
from jax.sharding import PartitionSpec as P

AXES = ("row", "grp")
PLANE = 8
SLOTS = 3
PLANE_SLOTS = 5
VMEM = pl.BlockSpec(memory_space=pltpu.VMEM)
SMEM = pl.BlockSpec(memory_space=pltpu.SMEM)
HBM = pl.BlockSpec(memory_space=pl.ANY)


def params(mib):
    return pltpu.CompilerParams(vmem_limit_bytes=mib * 2**20)


def held_in_vmem(x):
    return pltpu.with_memory_space_constraint(x, pltpu.VMEM)


def scan(ids, mine, fields):
    held = jnp.int32(0)
    found = [[jnp.int32(0)] * SLOTS for _ in fields]
    for j in range(ids.shape[0]):
        own = mine(ids[j])
        for f, field in enumerate(fields):
            for s in range(SLOTS):
                found[f][s] = jnp.where(own & (held == s), field(ids[j]), found[f][s])
        held = held + own.astype(jnp.int32)
    return found


def slot_of(ids, j, unit):
    slot = jnp.int32(0)
    for i in range(j):
        slot = slot + (ids[i] // unit == ids[j] // unit).astype(jnp.int32)
    return slot


def halves_kernel(ids, blocks, keep, give, sems):
    me = lax.axis_index(AXES)
    count = blocks.shape[0]
    core = me % 2
    at, owner = scan(
        ids, lambda i: i // (2 * count) == me // 2, [lambda i: i % count, lambda i: i // count + 1]
    )
    copies = []
    for s in range(SLOTS):
        for out, half in ((give, 1 - core), (keep, core)):
            copies.append(
                pltpu.make_async_copy(blocks.at[at[s], :, half], out.at[:, s], sems.at[len(copies)])
            )
    for s in range(SLOTS):

        @pl.when(owner[s] == me + 1)
        def _():
            copies[2 * s].start()
            copies[2 * s + 1].start()

    for s in range(SLOTS):

        @pl.when(owner[s] == me + 1)
        def _():
            copies[2 * s].wait()
            copies[2 * s + 1].wait()


def halves(ids, blocks, devices):
    count, tile, width = blocks.shape
    part = tile // devices
    groups = devices // PLANE
    shape = pltpu.VMEM((PLANE // 2, SLOTS, groups, part, width), blocks.dtype)
    return pl.pallas_call(
        halves_kernel,
        out_shape=[shape, shape],
        in_specs=[SMEM, HBM],
        out_specs=[VMEM, VMEM],
        scratch_shapes=[pltpu.SemaphoreType.DMA((2 * SLOTS,))],
        compiler_params=params(16),
    )(ids, blocks.reshape(count, PLANE // 2, 2, groups, part, width))


def merge_kernel(count, ids, keep, got, *outs):
    me = lax.axis_index(AXES)
    core, place = me % 2, me % PLANE // 2
    (cores,) = scan(
        ids, lambda i: i // (2 * count) == me // 2, [lambda i: i // count % 2]
    )
    for s in range(SLOTS):

        @pl.when(cores[s] == core)
        def _():
            for m, out in enumerate(outs):
                out[s] = keep[place ^ m, s]

        @pl.when(cores[s] != core)
        def _():
            for m, out in enumerate(outs):
                out[s] = got[place ^ m, s]


def merge(ids, keep, got, count):
    shape = pltpu.VMEM(keep.shape[1:], keep.dtype)
    return pl.pallas_call(
        functools.partial(merge_kernel, count),
        out_shape=[shape] * keep.shape[0],
        in_specs=[SMEM, VMEM, VMEM],
        out_specs=[VMEM] * keep.shape[0],
        compiler_params=params(16),
    )(ids, held_in_vmem(keep), held_in_vmem(got))


def sort_kernel(count, ids, *refs):
    near, outs = refs[: PLANE // 2], refs[PLANE // 2 :]
    me = lax.axis_index(AXES)
    group, place = me // PLANE, me % PLANE // 2
    for j in range(ids.shape[0]):
        owner = ids[j] // count
        slot = jnp.minimum(slot_of(ids, j, 2 * count), SLOTS - 1)
        to = jnp.minimum(slot_of(ids, j, PLANE * count), PLANE_SLOTS - 1)
        for m, ref in enumerate(near):

            @pl.when((owner // PLANE == group) & (owner % PLANE // 2 ^ place == m))
            def _():
                for g, out in enumerate(outs):
                    out[to] = ref[slot, group ^ g]


def sort(ids, near, count):
    _, groups, part, width = near[0].shape
    shape = pltpu.VMEM((PLANE_SLOTS, part, width), near[0].dtype)
    return pl.pallas_call(
        functools.partial(sort_kernel, count),
        out_shape=[shape] * groups,
        in_specs=[SMEM] + [VMEM] * len(near),
        out_specs=[VMEM] * groups,
        compiler_params=params(16),
    )(ids, *[held_in_vmem(x) for x in near])


def choose_kernel(count, ids, full, *refs):
    arrived, (spare, weight, out) = refs[:-3], refs[-3:]
    group = lax.axis_index(AXES) // PLANE
    parts = []
    for j in range(ids.shape[0]):
        at = group ^ ids[j] // (count * PLANE)
        slot = jnp.minimum(slot_of(ids, j, PLANE * count), PLANE_SLOTS - 1)
        part = arrived[0][slot].astype(jnp.float32)
        for g in range(1, len(arrived)):
            part = jnp.where(at == g, arrived[g][slot].astype(jnp.float32), part)
        parts.append(part)
    rows = jnp.concatenate(parts).astype(jnp.bfloat16)
    result = jnp.dot(rows, weight[...], preferred_element_type=jnp.float32)
    result = result.reshape(out.shape)
    out[...] = jnp.where(full[0] > 0, spare[...].astype(jnp.float32), result).astype(out.dtype)


def choose(ids, full, arrived, spare, weight, count):
    return pl.pallas_call(
        functools.partial(choose_kernel, count),
        out_shape=jax.ShapeDtypeStruct((ids.shape[0], *arrived[0].shape[1:]), arrived[0].dtype),
        in_specs=[SMEM, SMEM] + [VMEM] * (len(arrived) + 2),
        out_specs=VMEM,
        compiler_params=params(16),
    )(ids, full, *[held_in_vmem(x) for x in (*arrived, spare, weight)])


def send_kernel(ids, blocks, out, sems):
    me = lax.axis_index(AXES)
    count, _, groups, _, _ = blocks.shape
    slots = out.shape[1]
    held = jnp.int32(0)
    at = [jnp.int32(0)] * slots
    for j in range(ids.shape[0]):
        own = ids[j] // count == me
        for s in range(slots):
            at[s] = jnp.where(own & (held == s), ids[j] % count, at[s])
        held = held + own.astype(jnp.int32)
    copies = []
    for s in range(slots):
        for g in range(groups):
            copies.append(
                pltpu.make_async_copy(
                    blocks.at[at[s], :, g],
                    out.at[pl.ds(g * PLANE, PLANE), s],
                    sems.at[len(copies)],
                )
            )
            copies[-1].start()
    for copy in copies:
        copy.wait()


def send_layout(slots, ids, blocks, devices):
    count, tile, width = blocks.shape
    part = tile // devices
    groups = devices // PLANE
    return pl.pallas_call(
        send_kernel,
        out_shape=jax.ShapeDtypeStruct((devices, slots, part, width), blocks.dtype),
        in_specs=[SMEM, HBM],
        out_specs=VMEM,
        scratch_shapes=[pltpu.SemaphoreType.DMA((slots * groups,))],
        compiler_params=params(16),
    )(ids, blocks.reshape(count, PLANE, groups, part, width))


def rows_kernel(rows, counts, features, weight, *outs):
    slots, peers = rows.shape
    n = slots * peers
    groups = peers // PLANE
    me = lax.axis_index(AXES)
    slot = lax.broadcasted_iota(jnp.int32, (slots, peers), 0)
    wanted = jnp.where(slot < counts[...], rows[...], -1).astype(jnp.float32)
    at = lax.broadcasted_iota(jnp.int32, (n, peers), 0) // slots
    away = at % groups * PLANE + at // groups % (PLANE // 2) * 2 + at // (groups * PLANE // 2)
    peer = lax.broadcasted_iota(jnp.int32, (n, peers), 1)
    spread = jnp.where(away ^ peer == me, 1.0, 0.0)
    by_slot = lax.dot_general(
        spread, wanted, (((1,), (1,)), ((), ())), precision=lax.Precision.HIGHEST,
        preferred_element_type=jnp.float32,
    )
    line = lax.broadcasted_iota(jnp.int32, (n, slots), 0)
    slot = lax.broadcasted_iota(jnp.int32, (n, slots), 1)
    row = jnp.sum(jnp.where(line % slots == slot, by_slot, 0.0), axis=1, keepdims=True)
    row = jnp.round(row).astype(jnp.int32)
    hit = row == lax.broadcasted_iota(jnp.int32, (n, features.shape[0]), 1)
    picked = jnp.where(hit, 1.0, 0.0).astype(jnp.bfloat16)
    picked = jnp.dot(picked, features[...], preferred_element_type=jnp.float32)
    picked = jnp.dot(
        picked.astype(jnp.bfloat16), weight[...], preferred_element_type=jnp.float32
    )
    picked = picked.reshape(len(outs), *outs[0].shape)
    for core, out in enumerate(outs):
        out[...] = picked[core].astype(out.dtype)


def listed_rows(rows, counts, features, weight):
    peers, slots = rows.shape
    shape = pltpu.VMEM((PLANE // 2, peers // PLANE, slots, weight.shape[1]), features.dtype)
    return pl.pallas_call(
        rows_kernel,
        out_shape=[shape, shape],
        in_specs=[VMEM] * 4,
        out_specs=[VMEM] * 2,
        compiler_params=params(24),
    )(rows.T, counts.reshape(1, -1), features, held_in_vmem(weight))


def pick_kernel(count, ids, got, weight, out):
    n = ids.shape[0]
    parts = []
    for j in range(n):
        slot = jnp.minimum(slot_of(ids, j, count), got.shape[1] - 1)
        parts.append(got[ids[j] // count, slot].astype(jnp.float32))
    rows = jnp.concatenate(parts).astype(jnp.bfloat16)
    result = jnp.dot(rows, weight[...], preferred_element_type=jnp.float32)
    out[...] = result.reshape(out.shape).astype(out.dtype)


def pick(ids, got, weight, count):
    return pl.pallas_call(
        functools.partial(pick_kernel, count),
        out_shape=jax.ShapeDtypeStruct((ids.shape[0], *got.shape[2:]), got.dtype),
        in_specs=[SMEM, VMEM, VMEM],
        out_specs=VMEM,
        compiler_params=params(16),
    )(ids, got, held_in_vmem(weight))


def layer_kernel(group, meta, *refs):
    near, far = refs[:6], refs[6:10]
    listed, refs = refs[10:-7], refs[-7:]
    edge, sparse, bias, out, bands, rows_f32, rows_in = refs
    first = pl.program_id(0) * group
    blocks = pl.num_programs(0) * group
    _, tiles_per, tile, _ = edge.shape
    stripes, piece_rows, width = near[0].shape
    half = width // 2

    @pl.when(first == 0)
    def _():
        for i in range(PLANE):
            at = pl.multiple_of(meta[blocks * tiles_per + i] * piece_rows, piece_rows)
            for j in range(stripes):
                if i < 6:
                    bands[j, pl.ds(at, piece_rows), :] = near[i][j]
                else:
                    bands[j, pl.ds(at, piece_rows), :half] = far[i - 6][j]
                    bands[j, pl.ds(at, piece_rows), half:] = far[i - 4][j]
        me = lax.axis_index(AXES)
        slots = listed[0].shape[2]
        for g, ref in enumerate(listed):
            for m in range(PLANE // 2):
                for k in range(2):
                    at = pl.multiple_of((me ^ (g * PLANE + m * 2 + k)) * slots, slots)
                    rows_f32[pl.ds(at, slots), :] = ref[m, k].astype(jnp.float32)
        rows_in[...] = rows_f32[...].astype(rows_in.dtype)

    for k in range(group):
        rows = slice(k * tile, (k + 1) * tile)
        total = jnp.dot(sparse[rows], rows_in[...], preferred_element_type=jnp.float32)
        for t in range(tiles_per):
            band = bands[meta[(first + k) * tiles_per + t]]
            total += jnp.dot(edge[k, t], band, preferred_element_type=jnp.float32)
        out[rows] = jnp.maximum(total + bias[...], 0.0).astype(out.dtype)


def layer(meta, pieces, listed, edge, sparse, bias, group=4):
    blocks, tiles_per, tile, _ = edge.shape
    stripes, _, width = pieces[0].shape
    lines = sparse.shape[1]
    return pl.pallas_call(
        functools.partial(layer_kernel, group),
        out_shape=jax.ShapeDtypeStruct((blocks * tile, width), jnp.bfloat16),
        grid_spec=pltpu.PrefetchScalarGridSpec(
            num_scalar_prefetch=1,
            grid=(blocks // group,),
            in_specs=[VMEM] * (len(pieces) + len(listed))
            + [
                pl.BlockSpec((group, tiles_per, tile, tile), lambda b, m: (b, 0, 0, 0)),
                pl.BlockSpec((group * tile, lines), lambda b, m: (b, 0)),
                VMEM,
            ],
            out_specs=pl.BlockSpec((group * tile, width), lambda b, m: (b, 0)),
            scratch_shapes=[
                pltpu.VMEM((stripes, tile, width), jnp.bfloat16),
                pltpu.VMEM((lines, width), jnp.float32),
                pltpu.VMEM((lines, width), jnp.bfloat16),
            ],
        ),
        compiler_params=params(24),
        cost_estimate=pl.CostEstimate(
            flops=2 * blocks * tile * width * (tiles_per * tile + lines),
            bytes_accessed=2 * (edge.size + sparse.size + blocks * tile * width),
            transcendentals=0,
        ),
    )(
        meta,
        *[held_in_vmem(x) for x in (*pieces, *listed)],
        pltpu.with_memory_space_constraint(edge, pltpu.HBM),
        pltpu.with_memory_space_constraint(sparse, pltpu.HBM),
        held_in_vmem(bias),
    )


def on_device(features, edge, cols, ids, sparse_w, sparse_rows, sparse_counts, weight, bias):
    block_count, tiles_per, tile, _ = edge.shape
    width = features.shape[1]
    stripe_count = ids.shape[0]
    devices = sparse_rows.shape[1]
    groups = devices // PLANE
    me = lax.axis_index(AXES)
    group, place = me // PLANE, me % PLANE
    blocks = features.reshape(block_count, tile, width)

    def exchange(x):
        return lax.all_to_all(x, AXES, 0, 0, tiled=True)

    def swap(x, mask):
        return lax.ppermute(x, AXES, [(d, d ^ mask) for d in range(devices)])

    def scattered(slots):
        return pick(ids, exchange(send_layout(slots, ids, blocks, devices)), block_count)

    def load(unit):
        at = ids // unit
        return jnp.max(jnp.sum((at[:, None] == at[None, :]).astype(jnp.int32), axis=1))

    full = (load(2 * block_count) > SLOTS) | (load(PLANE * block_count) > PLANE_SLOTS)
    most = min(stripe_count, block_count)
    spare = lax.cond(
        full,
        lambda: pick(ids, exchange(send_layout(most, ids, blocks, devices)), weight, block_count),
        lambda: jnp.zeros((stripe_count, tile // devices, width), features.dtype),
    )
    full = full.astype(jnp.int32)[None]

    keep, give = halves(ids, blocks, devices)
    sent = merge(ids, keep, swap(give, 1), block_count)
    near = [sent[0]] + [swap(x, 2 * m) for m, x in enumerate(sent) if m > 0]

    features, _ = lax.optimization_barrier((features, sent[0]))
    for_own, for_pair = listed_rows(sparse_rows[0], sparse_counts[0], features, weight)
    near[1], for_pair = lax.optimization_barrier((near[1], for_pair))
    from_pair = swap(for_pair, 1)

    near[2], spare = lax.optimization_barrier((near[2], spare))
    over = sort(ids, near, block_count)
    arrived = [over[0]] + [swap(x, PLANE * g) for g, x in enumerate(over) if g > 0]

    from_pair, _ = lax.optimization_barrier((from_pair, over[0]))
    both = jnp.stack([for_own, from_pair]).reshape(2, 2, 2, *for_own.shape[1:])
    across = swap(both[:, 1], 4)

    arrived[-1], across = lax.optimization_barrier((arrived[-1], across))

    held = choose(ids, full, arrived, spare, weight, block_count)

    parts = [held] + [swap(held, PLANE * g) for g in range(1, groups)]
    across, _ = lax.optimization_barrier((across, held))
    turned = swap(jnp.stack([both[:, 0, 1], across[:, 1]]), 2)
    listed = [both[:, 0, 0], turned[0], across[:, 0], turned[1]]
    ordered = [lax.select_n(group, *[parts[q ^ g] for g in range(groups)]) for q in range(groups)]
    own = jnp.concatenate(ordered, axis=1)

    own, *listed = lax.optimization_barrier((own, *listed))
    x, y = swap(own, 4), swap(own, 2)
    listed = [jnp.stack([r[:, g] for r in listed]) for g in range(groups)]
    listed = [swap(r, PLANE * g) if g else r for g, r in enumerate(listed)]
    half = width // 2
    left, right = swap(x[:, :, :half], 2), swap(y[:, :, half:], 4)
    pieces = [own, swap(own, 1), y, swap(y, 1), x, swap(x, 1)]
    pieces += [left, swap(left, 1), right, swap(right, 1)]

    meta = jnp.concatenate(
        [cols.reshape(-1), place ^ jnp.arange(PLANE, dtype=jnp.int32)]
    ).astype(jnp.int32)
    return layer(meta, pieces, listed, edge, sparse_w, bias.reshape(1, -1))


def solution(mesh):
    placed = (
        P(AXES, None),
        P(AXES, None, None, None),
        P(AXES, None),
        P(),
        P(AXES, None),
        P(AXES, None, None),
        P(AXES, None),
        P(),
        P(),
    )
    return jax.shard_map(
        on_device, mesh=mesh, in_specs=placed, out_specs=P(AXES, None), check_vma=False
    )
```

```python
import functools

import jax
import jax.numpy as jnp
from jax import lax
from jax.experimental import pallas as pl
from jax.experimental.pallas import tpu as pltpu
from jax.sharding import PartitionSpec as P

AXES = ("row", "grp")
PLANE = 8
SLOTS = 3
PLANE_SLOTS = 5
VMEM = pl.BlockSpec(memory_space=pltpu.VMEM)
SMEM = pl.BlockSpec(memory_space=pltpu.SMEM)
HBM = pl.BlockSpec(memory_space=pl.ANY)


def params(mib):
    return pltpu.CompilerParams(vmem_limit_bytes=mib * 2**20)


def held_in_vmem(x):
    return pltpu.with_memory_space_constraint(x, pltpu.VMEM)


def scan(ids, mine, fields):
    held = jnp.int32(0)
    found = [[jnp.int32(0)] * SLOTS for _ in fields]
    for j in range(ids.shape[0]):
        own = mine(ids[j])
        for f, field in enumerate(fields):
            for s in range(SLOTS):
                found[f][s] = jnp.where(own & (held == s), field(ids[j]), found[f][s])
        held = held + own.astype(jnp.int32)
    return found


def slot_of(ids, j, unit):
    slot = jnp.int32(0)
    for i in range(j):
        slot = slot + (ids[i] // unit == ids[j] // unit).astype(jnp.int32)
    return slot


def halves_kernel(ids, blocks, keep, give, sems):
    me = lax.axis_index(AXES)
    count = blocks.shape[0]
    core = me % 2
    at, owner = scan(
        ids, lambda i: i // (2 * count) == me // 2, [lambda i: i % count, lambda i: i // count + 1]
    )
    copies = []
    for s in range(SLOTS):
        for out, half in ((give, 1 - core), (keep, core)):
            copies.append(
                pltpu.make_async_copy(blocks.at[at[s], :, half], out.at[:, s], sems.at[len(copies)])
            )
    for s in range(SLOTS):

        @pl.when(owner[s] == me + 1)
        def _():
            copies[2 * s].start()
            copies[2 * s + 1].start()

    for s in range(SLOTS):

        @pl.when(owner[s] == me + 1)
        def _():
            copies[2 * s].wait()
            copies[2 * s + 1].wait()


def halves(ids, blocks, devices):
    count, tile, width = blocks.shape
    part = tile // devices
    groups = devices // PLANE
    shape = pltpu.VMEM((PLANE // 2, SLOTS, groups, part, width), blocks.dtype)
    return pl.pallas_call(
        halves_kernel,
        out_shape=[shape, shape],
        in_specs=[SMEM, HBM],
        out_specs=[VMEM, VMEM],
        scratch_shapes=[pltpu.SemaphoreType.DMA((2 * SLOTS,))],
        compiler_params=params(16),
    )(ids, blocks.reshape(count, PLANE // 2, 2, groups, part, width))


def merge_kernel(count, ids, keep, got, *outs):
    me = lax.axis_index(AXES)
    core, place = me % 2, me % PLANE // 2
    (cores,) = scan(
        ids, lambda i: i // (2 * count) == me // 2, [lambda i: i // count % 2]
    )
    for s in range(SLOTS):

        @pl.when(cores[s] == core)
        def _():
            for m, out in enumerate(outs):
                out[s] = keep[place ^ m, s]

        @pl.when(cores[s] != core)
        def _():
            for m, out in enumerate(outs):
                out[s] = got[place ^ m, s]


def merge(ids, keep, got, count):
    shape = pltpu.VMEM(keep.shape[1:], keep.dtype)
    return pl.pallas_call(
        functools.partial(merge_kernel, count),
        out_shape=[shape] * keep.shape[0],
        in_specs=[SMEM, VMEM, VMEM],
        out_specs=[VMEM] * keep.shape[0],
        compiler_params=params(16),
    )(ids, held_in_vmem(keep), held_in_vmem(got))


def sort_kernel(count, ids, *refs):
    near, outs = refs[: PLANE // 2], refs[PLANE // 2 :]
    me = lax.axis_index(AXES)
    group, place = me // PLANE, me % PLANE // 2
    for j in range(ids.shape[0]):
        owner = ids[j] // count
        slot = jnp.minimum(slot_of(ids, j, 2 * count), SLOTS - 1)
        to = jnp.minimum(slot_of(ids, j, PLANE * count), PLANE_SLOTS - 1)

        @pl.when(owner // PLANE == group)
        def _():
            for m, ref in enumerate(near):

                @pl.when(owner % PLANE // 2 ^ place == m)
                def _():
                    for g, out in enumerate(outs):
                        out[to] = ref[slot, group ^ g]


def sort(ids, near, count):
    _, groups, part, width = near[0].shape
    shape = pltpu.VMEM((PLANE_SLOTS, part, width), near[0].dtype)
    return pl.pallas_call(
        functools.partial(sort_kernel, count),
        out_shape=[shape] * groups,
        in_specs=[SMEM] + [VMEM] * len(near),
        out_specs=[VMEM] * groups,
        compiler_params=params(16),
    )(ids, *[held_in_vmem(x) for x in near])


def choose_kernel(count, ids, full, *refs):
    arrived, (spare, weight, out) = refs[:-3], refs[-3:]
    group = lax.axis_index(AXES) // PLANE
    parts = []
    for j in range(ids.shape[0]):
        at = group ^ ids[j] // (count * PLANE)
        slot = jnp.minimum(slot_of(ids, j, PLANE * count), PLANE_SLOTS - 1)
        part = arrived[0][slot].astype(jnp.float32)
        for g in range(1, len(arrived)):
            part = jnp.where(at == g, arrived[g][slot].astype(jnp.float32), part)
        parts.append(part)
    rows = jnp.concatenate(parts).astype(jnp.bfloat16)
    result = jnp.dot(rows, weight[...], preferred_element_type=jnp.float32)
    result = result.reshape(out.shape)
    out[...] = jnp.where(full[0] > 0, spare[...].astype(jnp.float32), result).astype(out.dtype)


def choose(ids, full, arrived, spare, weight, count):
    return pl.pallas_call(
        functools.partial(choose_kernel, count),
        out_shape=jax.ShapeDtypeStruct((ids.shape[0], *arrived[0].shape[1:]), arrived[0].dtype),
        in_specs=[SMEM, SMEM] + [VMEM] * (len(arrived) + 2),
        out_specs=VMEM,
        compiler_params=params(16),
    )(ids, full, *[held_in_vmem(x) for x in (*arrived, spare, weight)])


def send_kernel(ids, blocks, out, sems):
    me = lax.axis_index(AXES)
    count, _, groups, _, _ = blocks.shape
    slots = out.shape[1]
    held = jnp.int32(0)
    at = [jnp.int32(0)] * slots
    for j in range(ids.shape[0]):
        own = ids[j] // count == me
        for s in range(slots):
            at[s] = jnp.where(own & (held == s), ids[j] % count, at[s])
        held = held + own.astype(jnp.int32)
    copies = []
    for s in range(slots):
        for g in range(groups):
            copies.append(
                pltpu.make_async_copy(
                    blocks.at[at[s], :, g],
                    out.at[pl.ds(g * PLANE, PLANE), s],
                    sems.at[len(copies)],
                )
            )
            copies[-1].start()
    for copy in copies:
        copy.wait()


def send_layout(slots, ids, blocks, devices):
    count, tile, width = blocks.shape
    part = tile // devices
    groups = devices // PLANE
    return pl.pallas_call(
        send_kernel,
        out_shape=jax.ShapeDtypeStruct((devices, slots, part, width), blocks.dtype),
        in_specs=[SMEM, HBM],
        out_specs=VMEM,
        scratch_shapes=[pltpu.SemaphoreType.DMA((slots * groups,))],
        compiler_params=params(16),
    )(ids, blocks.reshape(count, PLANE, groups, part, width))


def rows_kernel(rows, counts, features, weight, *outs):
    slots, peers = rows.shape
    n = slots * peers
    groups = peers // PLANE
    me = lax.axis_index(AXES)
    slot = lax.broadcasted_iota(jnp.int32, (slots, peers), 0)
    wanted = jnp.where(slot < counts[...], rows[...], -1).astype(jnp.float32)
    at = lax.broadcasted_iota(jnp.int32, (n, peers), 0) // slots
    away = at % groups * PLANE + at // groups % (PLANE // 2) * 2 + at // (groups * PLANE // 2)
    peer = lax.broadcasted_iota(jnp.int32, (n, peers), 1)
    spread = jnp.where(away ^ peer == me, 1.0, 0.0)
    by_slot = lax.dot_general(
        spread, wanted, (((1,), (1,)), ((), ())), precision=lax.Precision.HIGHEST,
        preferred_element_type=jnp.float32,
    )
    line = lax.broadcasted_iota(jnp.int32, (n, slots), 0)
    slot = lax.broadcasted_iota(jnp.int32, (n, slots), 1)
    row = jnp.sum(jnp.where(line % slots == slot, by_slot, 0.0), axis=1, keepdims=True)
    row = jnp.round(row).astype(jnp.int32)
    hit = row == lax.broadcasted_iota(jnp.int32, (n, features.shape[0]), 1)
    picked = jnp.where(hit, 1.0, 0.0).astype(jnp.bfloat16)
    picked = jnp.dot(picked, features[...], preferred_element_type=jnp.float32)
    picked = jnp.dot(
        picked.astype(jnp.bfloat16), weight[...], preferred_element_type=jnp.float32
    )
    picked = picked.reshape(len(outs), *outs[0].shape)
    for core, out in enumerate(outs):
        out[...] = picked[core].astype(out.dtype)


def listed_rows(rows, counts, features, weight):
    peers, slots = rows.shape
    shape = pltpu.VMEM((PLANE // 2, peers // PLANE, slots, weight.shape[1]), features.dtype)
    return pl.pallas_call(
        rows_kernel,
        out_shape=[shape, shape],
        in_specs=[VMEM] * 4,
        out_specs=[VMEM] * 2,
        compiler_params=params(24),
    )(rows.T, counts.reshape(1, -1), features, held_in_vmem(weight))


def pick_kernel(count, ids, got, weight, out):
    n = ids.shape[0]
    parts = []
    for j in range(n):
        slot = jnp.minimum(slot_of(ids, j, count), got.shape[1] - 1)
        parts.append(got[ids[j] // count, slot].astype(jnp.float32))
    rows = jnp.concatenate(parts).astype(jnp.bfloat16)
    result = jnp.dot(rows, weight[...], preferred_element_type=jnp.float32)
    out[...] = result.reshape(out.shape).astype(out.dtype)


def pick(ids, got, weight, count):
    return pl.pallas_call(
        functools.partial(pick_kernel, count),
        out_shape=jax.ShapeDtypeStruct((ids.shape[0], *got.shape[2:]), got.dtype),
        in_specs=[SMEM, VMEM, VMEM],
        out_specs=VMEM,
        compiler_params=params(16),
    )(ids, got, held_in_vmem(weight))


def layer_kernel(group, meta, *refs):
    near, far = refs[:6], refs[6:10]
    listed, refs = refs[10:-7], refs[-7:]
    edge, sparse, bias, out, bands, rows_f32, rows_in = refs
    first = pl.program_id(0) * group
    blocks = pl.num_programs(0) * group
    _, tiles_per, tile, _ = edge.shape
    stripes, piece_rows, width = near[0].shape
    half = width // 2

    @pl.when(first == 0)
    def _():
        for i in range(PLANE):
            at = pl.multiple_of(meta[blocks * tiles_per + i] * piece_rows, piece_rows)
            for j in range(stripes):
                if i < 6:
                    bands[j, pl.ds(at, piece_rows), :] = near[i][j]
                else:
                    bands[j, pl.ds(at, piece_rows), :half] = far[i - 6][j]
                    bands[j, pl.ds(at, piece_rows), half:] = far[i - 4][j]
        me = lax.axis_index(AXES)
        slots = listed[0].shape[2]
        for g, ref in enumerate(listed):
            for m in range(PLANE // 2):
                for k in range(2):
                    at = pl.multiple_of((me ^ (g * PLANE + m * 2 + k)) * slots, slots)
                    rows_f32[pl.ds(at, slots), :] = ref[m, k].astype(jnp.float32)
        rows_in[...] = rows_f32[...].astype(rows_in.dtype)

    for k in range(group):
        rows = slice(k * tile, (k + 1) * tile)
        total = jnp.dot(sparse[rows], rows_in[...], preferred_element_type=jnp.float32)
        for t in range(tiles_per):
            band = bands[meta[(first + k) * tiles_per + t]]
            total += jnp.dot(edge[k, t], band, preferred_element_type=jnp.float32)
        out[rows] = jnp.maximum(total + bias[...], 0.0).astype(out.dtype)


def layer(meta, pieces, listed, edge, sparse, bias, group=4):
    blocks, tiles_per, tile, _ = edge.shape
    stripes, _, width = pieces[0].shape
    lines = sparse.shape[1]
    return pl.pallas_call(
        functools.partial(layer_kernel, group),
        out_shape=jax.ShapeDtypeStruct((blocks * tile, width), jnp.bfloat16),
        grid_spec=pltpu.PrefetchScalarGridSpec(
            num_scalar_prefetch=1,
            grid=(blocks // group,),
            in_specs=[VMEM] * (len(pieces) + len(listed))
            + [
                pl.BlockSpec((group, tiles_per, tile, tile), lambda b, m: (b, 0, 0, 0)),
                pl.BlockSpec((group * tile, lines), lambda b, m: (b, 0)),
                VMEM,
            ],
            out_specs=pl.BlockSpec((group * tile, width), lambda b, m: (b, 0)),
            scratch_shapes=[
                pltpu.VMEM((stripes, tile, width), jnp.bfloat16),
                pltpu.VMEM((lines, width), jnp.float32),
                pltpu.VMEM((lines, width), jnp.bfloat16),
            ],
        ),
        compiler_params=params(24),
        cost_estimate=pl.CostEstimate(
            flops=2 * blocks * tile * width * (tiles_per * tile + lines),
            bytes_accessed=2 * (edge.size + sparse.size + blocks * tile * width),
            transcendentals=0,
        ),
    )(
        meta,
        *[held_in_vmem(x) for x in (*pieces, *listed)],
        pltpu.with_memory_space_constraint(edge, pltpu.HBM),
        pltpu.with_memory_space_constraint(sparse, pltpu.HBM),
        held_in_vmem(bias),
    )


def on_device(features, edge, cols, ids, sparse_w, sparse_rows, sparse_counts, weight, bias):
    block_count, tiles_per, tile, _ = edge.shape
    width = features.shape[1]
    stripe_count = ids.shape[0]
    devices = sparse_rows.shape[1]
    groups = devices // PLANE
    me = lax.axis_index(AXES)
    group, place = me // PLANE, me % PLANE
    blocks = features.reshape(block_count, tile, width)

    def exchange(x):
        return lax.all_to_all(x, AXES, 0, 0, tiled=True)

    def swap(x, mask):
        return lax.ppermute(x, AXES, [(d, d ^ mask) for d in range(devices)])

    def scattered(slots):
        return pick(ids, exchange(send_layout(slots, ids, blocks, devices)), block_count)

    def load(unit):
        at = ids // unit
        return jnp.max(jnp.sum((at[:, None] == at[None, :]).astype(jnp.int32), axis=1))

    full = (load(2 * block_count) > SLOTS) | (load(PLANE * block_count) > PLANE_SLOTS)
    most = min(stripe_count, block_count)
    spare = lax.cond(
        full,
        lambda: pick(ids, exchange(send_layout(most, ids, blocks, devices)), weight, block_count),
        lambda: jnp.zeros((stripe_count, tile // devices, width), features.dtype),
    )
    full = full.astype(jnp.int32)[None]

    keep, give = halves(ids, blocks, devices)
    sent = merge(ids, keep, swap(give, 1), block_count)
    near = [sent[0]] + [swap(x, 2 * m) for m, x in enumerate(sent) if m > 0]

    features, _ = lax.optimization_barrier((features, sent[0]))
    for_own, for_pair = listed_rows(sparse_rows[0], sparse_counts[0], features, weight)
    near[1], for_pair = lax.optimization_barrier((near[1], for_pair))
    from_pair = swap(for_pair, 1)

    near[2], spare = lax.optimization_barrier((near[2], spare))
    over = sort(ids, near, block_count)
    arrived = [over[0]] + [swap(x, PLANE * g) for g, x in enumerate(over) if g > 0]

    from_pair, _ = lax.optimization_barrier((from_pair, over[0]))
    both = jnp.stack([for_own, from_pair]).reshape(2, 2, 2, *for_own.shape[1:])
    across = swap(both[:, 1], 4)

    arrived[-1], across = lax.optimization_barrier((arrived[-1], across))

    held = choose(ids, full, arrived, spare, weight, block_count)

    parts = [held] + [swap(held, PLANE * g) for g in range(1, groups)]
    across, _ = lax.optimization_barrier((across, held))
    turned = swap(jnp.stack([both[:, 0, 1], across[:, 1]]), 2)
    listed = [both[:, 0, 0], turned[0], across[:, 0], turned[1]]
    ordered = [lax.select_n(group, *[parts[q ^ g] for g in range(groups)]) for q in range(groups)]
    own = jnp.concatenate(ordered, axis=1)

    own, *listed = lax.optimization_barrier((own, *listed))
    x, y = swap(own, 4), swap(own, 2)
    listed = [jnp.stack([r[:, g] for r in listed]) for g in range(groups)]
    listed = [swap(r, PLANE * g) if g else r for g, r in enumerate(listed)]
    half = width // 2
    left, right = swap(x[:, :, :half], 2), swap(y[:, :, half:], 4)
    pieces = [own, swap(own, 1), y, swap(y, 1), x, swap(x, 1)]
    pieces += [left, swap(left, 1), right, swap(right, 1)]

    meta = jnp.concatenate(
        [cols.reshape(-1), place ^ jnp.arange(PLANE, dtype=jnp.int32)]
    ).astype(jnp.int32)
    return layer(meta, pieces, listed, edge, sparse_w, bias.reshape(1, -1))


def solution(mesh):
    placed = (
        P(AXES, None),
        P(AXES, None, None, None),
        P(AXES, None),
        P(),
        P(AXES, None),
        P(AXES, None, None),
        P(AXES, None),
        P(),
        P(),
    )
    return jax.shard_map(
        on_device, mesh=mesh, in_specs=placed, out_specs=P(AXES, None), check_vma=False
    )
```

```python
import functools

import jax
import jax.numpy as jnp
from jax import lax
from jax.experimental import pallas as pl
from jax.experimental.pallas import tpu as pltpu
from jax.sharding import PartitionSpec as P

AXES = ("row", "grp")
PLANE = 8
SLOTS = 3
PLANE_SLOTS = 5
VMEM = pl.BlockSpec(memory_space=pltpu.VMEM)
SMEM = pl.BlockSpec(memory_space=pltpu.SMEM)
HBM = pl.BlockSpec(memory_space=pl.ANY)


def params(mib):
    return pltpu.CompilerParams(vmem_limit_bytes=mib * 2**20)


def held_in_vmem(x):
    return pltpu.with_memory_space_constraint(x, pltpu.VMEM)


def scan(ids, mine, fields):
    held = jnp.int32(0)
    found = [[jnp.int32(0)] * SLOTS for _ in fields]
    for j in range(ids.shape[0]):
        own = mine(ids[j])
        for f, field in enumerate(fields):
            for s in range(SLOTS):
                found[f][s] = jnp.where(own & (held == s), field(ids[j]), found[f][s])
        held = held + own.astype(jnp.int32)
    return found


def slot_of(ids, j, unit):
    slot = jnp.int32(0)
    for i in range(j):
        slot = slot + (ids[i] // unit == ids[j] // unit).astype(jnp.int32)
    return slot


def halves_kernel(ids, blocks, keep, give, sems):
    me = lax.axis_index(AXES)
    count = blocks.shape[0]
    core = me % 2
    at, owner = scan(
        ids, lambda i: i // (2 * count) == me // 2, [lambda i: i % count, lambda i: i // count + 1]
    )
    copies = []
    for s in range(SLOTS):
        for out, half in ((give, 1 - core), (keep, core)):
            copies.append(
                pltpu.make_async_copy(blocks.at[at[s], :, half], out.at[:, s], sems.at[len(copies)])
            )
    for s in range(SLOTS):

        @pl.when(owner[s] == me + 1)
        def _():
            copies[2 * s].start()
            copies[2 * s + 1].start()

    for s in range(SLOTS):

        @pl.when(owner[s] == me + 1)
        def _():
            copies[2 * s].wait()
            copies[2 * s + 1].wait()


def halves(ids, blocks, devices):
    count, tile, width = blocks.shape
    part = tile // devices
    groups = devices // PLANE
    shape = pltpu.VMEM((PLANE // 2, SLOTS, groups, part, width), blocks.dtype)
    return pl.pallas_call(
        halves_kernel,
        out_shape=[shape, shape],
        in_specs=[SMEM, HBM],
        out_specs=[VMEM, VMEM],
        scratch_shapes=[pltpu.SemaphoreType.DMA((2 * SLOTS,))],
        compiler_params=params(16),
    )(ids, blocks.reshape(count, PLANE // 2, 2, groups, part, width))


def merge_kernel(count, ids, keep, got, *outs):
    me = lax.axis_index(AXES)
    place = me % PLANE // 2
    (owner,) = scan(ids, lambda i: i // (2 * count) == me // 2, [lambda i: i // count + 1])
    for s in range(SLOTS):

        @pl.when(owner[s] == me + 1)
        def _():
            for m, out in enumerate(outs):
                out[s] = keep[place ^ m, s]

        @pl.when((owner[s] > 0) & (owner[s] != me + 1))
        def _():
            for m, out in enumerate(outs):
                out[s] = got[place ^ m, s]


def merge(ids, keep, got, count):
    shape = pltpu.VMEM(keep.shape[1:], keep.dtype)
    return pl.pallas_call(
        functools.partial(merge_kernel, count),
        out_shape=[shape] * keep.shape[0],
        in_specs=[SMEM, VMEM, VMEM],
        out_specs=[VMEM] * keep.shape[0],
        compiler_params=params(16),
    )(ids, held_in_vmem(keep), held_in_vmem(got))


def sort_kernel(count, ids, *refs):
    near, outs = refs[: PLANE // 2], refs[PLANE // 2 :]
    me = lax.axis_index(AXES)
    group, place = me // PLANE, me % PLANE // 2
    for j in range(ids.shape[0]):
        owner = ids[j] // count
        slot = jnp.minimum(slot_of(ids, j, 2 * count), SLOTS - 1)
        to = jnp.minimum(slot_of(ids, j, PLANE * count), PLANE_SLOTS - 1)
        for m, ref in enumerate(near):

            @pl.when((owner // PLANE == group) & (owner % PLANE // 2 ^ place == m))
            def _():
                for g, out in enumerate(outs):
                    out[to] = ref[slot, group ^ g]


def sort(ids, near, count):
    _, groups, part, width = near[0].shape
    shape = pltpu.VMEM((PLANE_SLOTS, part, width), near[0].dtype)
    return pl.pallas_call(
        functools.partial(sort_kernel, count),
        out_shape=[shape] * groups,
        in_specs=[SMEM] + [VMEM] * len(near),
        out_specs=[VMEM] * groups,
        compiler_params=params(16),
    )(ids, *[held_in_vmem(x) for x in near])


def choose_kernel(count, ids, full, *refs):
    arrived, (spare, weight, out) = refs[:-3], refs[-3:]
    group = lax.axis_index(AXES) // PLANE
    parts = []
    for j in range(ids.shape[0]):
        at = group ^ ids[j] // (count * PLANE)
        slot = jnp.minimum(slot_of(ids, j, PLANE * count), PLANE_SLOTS - 1)
        part = arrived[0][slot].astype(jnp.float32)
        for g in range(1, len(arrived)):
            part = jnp.where(at == g, arrived[g][slot].astype(jnp.float32), part)
        parts.append(part)
    rows = jnp.concatenate(parts).astype(jnp.bfloat16)
    result = jnp.dot(rows, weight[...], preferred_element_type=jnp.float32)
    result = result.reshape(out.shape)
    out[...] = jnp.where(full[0] > 0, spare[...].astype(jnp.float32), result).astype(out.dtype)


def choose(ids, full, arrived, spare, weight, count):
    return pl.pallas_call(
        functools.partial(choose_kernel, count),
        out_shape=jax.ShapeDtypeStruct((ids.shape[0], *arrived[0].shape[1:]), arrived[0].dtype),
        in_specs=[SMEM, SMEM] + [VMEM] * (len(arrived) + 2),
        out_specs=VMEM,
        compiler_params=params(16),
    )(ids, full, *[held_in_vmem(x) for x in (*arrived, spare, weight)])


def send_kernel(ids, blocks, out, sems):
    me = lax.axis_index(AXES)
    count, _, groups, _, _ = blocks.shape
    slots = out.shape[1]
    held = jnp.int32(0)
    at = [jnp.int32(0)] * slots
    for j in range(ids.shape[0]):
        own = ids[j] // count == me
        for s in range(slots):
            at[s] = jnp.where(own & (held == s), ids[j] % count, at[s])
        held = held + own.astype(jnp.int32)
    copies = []
    for s in range(slots):
        for g in range(groups):
            copies.append(
                pltpu.make_async_copy(
                    blocks.at[at[s], :, g],
                    out.at[pl.ds(g * PLANE, PLANE), s],
                    sems.at[len(copies)],
                )
            )
            copies[-1].start()
    for copy in copies:
        copy.wait()


def send_layout(slots, ids, blocks, devices):
    count, tile, width = blocks.shape
    part = tile // devices
    groups = devices // PLANE
    return pl.pallas_call(
        send_kernel,
        out_shape=jax.ShapeDtypeStruct((devices, slots, part, width), blocks.dtype),
        in_specs=[SMEM, HBM],
        out_specs=VMEM,
        scratch_shapes=[pltpu.SemaphoreType.DMA((slots * groups,))],
        compiler_params=params(16),
    )(ids, blocks.reshape(count, PLANE, groups, part, width))


def rows_kernel(rows, counts, features, weight, *outs):
    slots, peers = rows.shape
    n = slots * peers
    groups = peers // PLANE
    me = lax.axis_index(AXES)
    slot = lax.broadcasted_iota(jnp.int32, (slots, peers), 0)
    wanted = jnp.where(slot < counts[...], rows[...], -1).astype(jnp.float32)
    at = lax.broadcasted_iota(jnp.int32, (n, peers), 0) // slots
    away = at % groups * PLANE + at // groups % (PLANE // 2) * 2 + at // (groups * PLANE // 2)
    peer = lax.broadcasted_iota(jnp.int32, (n, peers), 1)
    spread = jnp.where(away ^ peer == me, 1.0, 0.0)
    by_slot = lax.dot_general(
        spread, wanted, (((1,), (1,)), ((), ())), precision=lax.Precision.HIGHEST,
        preferred_element_type=jnp.float32,
    )
    line = lax.broadcasted_iota(jnp.int32, (n, slots), 0)
    slot = lax.broadcasted_iota(jnp.int32, (n, slots), 1)
    row = jnp.sum(jnp.where(line % slots == slot, by_slot, 0.0), axis=1, keepdims=True)
    row = jnp.round(row).astype(jnp.int32)
    hit = row == lax.broadcasted_iota(jnp.int32, (n, features.shape[0]), 1)
    picked = jnp.where(hit, 1.0, 0.0).astype(jnp.bfloat16)
    picked = jnp.dot(picked, features[...], preferred_element_type=jnp.float32)
    picked = jnp.dot(
        picked.astype(jnp.bfloat16), weight[...], preferred_element_type=jnp.float32
    )
    picked = picked.reshape(len(outs), *outs[0].shape)
    for core, out in enumerate(outs):
        out[...] = picked[core].astype(out.dtype)


def listed_rows(rows, counts, features, weight):
    peers, slots = rows.shape
    shape = pltpu.VMEM((PLANE // 2, peers // PLANE, slots, weight.shape[1]), features.dtype)
    return pl.pallas_call(
        rows_kernel,
        out_shape=[shape, shape],
        in_specs=[VMEM] * 4,
        out_specs=[VMEM] * 2,
        compiler_params=params(24),
    )(rows.T, counts.reshape(1, -1), features, held_in_vmem(weight))


def pick_kernel(count, ids, got, weight, out):
    n = ids.shape[0]
    parts = []
    for j in range(n):
        slot = jnp.minimum(slot_of(ids, j, count), got.shape[1] - 1)
        parts.append(got[ids[j] // count, slot].astype(jnp.float32))
    rows = jnp.concatenate(parts).astype(jnp.bfloat16)
    result = jnp.dot(rows, weight[...], preferred_element_type=jnp.float32)
    out[...] = result.reshape(out.shape).astype(out.dtype)


def pick(ids, got, weight, count):
    return pl.pallas_call(
        functools.partial(pick_kernel, count),
        out_shape=jax.ShapeDtypeStruct((ids.shape[0], *got.shape[2:]), got.dtype),
        in_specs=[SMEM, VMEM, VMEM],
        out_specs=VMEM,
        compiler_params=params(16),
    )(ids, got, held_in_vmem(weight))


def layer_kernel(group, meta, *refs):
    near, far = refs[:6], refs[6:10]
    listed, refs = refs[10:-7], refs[-7:]
    edge, sparse, bias, out, bands, rows_f32, rows_in = refs
    first = pl.program_id(0) * group
    blocks = pl.num_programs(0) * group
    _, tiles_per, tile, _ = edge.shape
    stripes, piece_rows, width = near[0].shape
    half = width // 2

    @pl.when(first == 0)
    def _():
        for i in range(PLANE):
            at = pl.multiple_of(meta[blocks * tiles_per + i] * piece_rows, piece_rows)
            for j in range(stripes):
                if i < 6:
                    bands[j, pl.ds(at, piece_rows), :] = near[i][j]
                else:
                    bands[j, pl.ds(at, piece_rows), :half] = far[i - 6][j]
                    bands[j, pl.ds(at, piece_rows), half:] = far[i - 4][j]
        me = lax.axis_index(AXES)
        slots = listed[0].shape[2]
        for g, ref in enumerate(listed):
            for m in range(PLANE // 2):
                for k in range(2):
                    at = pl.multiple_of((me ^ (g * PLANE + m * 2 + k)) * slots, slots)
                    rows_f32[pl.ds(at, slots), :] = ref[m, k].astype(jnp.float32)
        rows_in[...] = rows_f32[...].astype(rows_in.dtype)

    for k in range(group):
        rows = slice(k * tile, (k + 1) * tile)
        total = jnp.dot(sparse[rows], rows_in[...], preferred_element_type=jnp.float32)
        for t in range(tiles_per):
            band = bands[meta[(first + k) * tiles_per + t]]
            total += jnp.dot(edge[k, t], band, preferred_element_type=jnp.float32)
        out[rows] = jnp.maximum(total + bias[...], 0.0).astype(out.dtype)


def layer(meta, pieces, listed, edge, sparse, bias, group=4):
    blocks, tiles_per, tile, _ = edge.shape
    stripes, _, width = pieces[0].shape
    lines = sparse.shape[1]
    return pl.pallas_call(
        functools.partial(layer_kernel, group),
        out_shape=jax.ShapeDtypeStruct((blocks * tile, width), jnp.bfloat16),
        grid_spec=pltpu.PrefetchScalarGridSpec(
            num_scalar_prefetch=1,
            grid=(blocks // group,),
            in_specs=[VMEM] * (len(pieces) + len(listed))
            + [
                pl.BlockSpec((group, tiles_per, tile, tile), lambda b, m: (b, 0, 0, 0)),
                pl.BlockSpec((group * tile, lines), lambda b, m: (b, 0)),
                VMEM,
            ],
            out_specs=pl.BlockSpec((group * tile, width), lambda b, m: (b, 0)),
            scratch_shapes=[
                pltpu.VMEM((stripes, tile, width), jnp.bfloat16),
                pltpu.VMEM((lines, width), jnp.float32),
                pltpu.VMEM((lines, width), jnp.bfloat16),
            ],
        ),
        compiler_params=params(24),
        cost_estimate=pl.CostEstimate(
            flops=2 * blocks * tile * width * (tiles_per * tile + lines),
            bytes_accessed=2 * (edge.size + sparse.size + blocks * tile * width),
            transcendentals=0,
        ),
    )(
        meta,
        *[held_in_vmem(x) for x in (*pieces, *listed)],
        pltpu.with_memory_space_constraint(edge, pltpu.HBM),
        pltpu.with_memory_space_constraint(sparse, pltpu.HBM),
        held_in_vmem(bias),
    )


def on_device(features, edge, cols, ids, sparse_w, sparse_rows, sparse_counts, weight, bias):
    block_count, tiles_per, tile, _ = edge.shape
    width = features.shape[1]
    stripe_count = ids.shape[0]
    devices = sparse_rows.shape[1]
    groups = devices // PLANE
    me = lax.axis_index(AXES)
    group, place = me // PLANE, me % PLANE
    blocks = features.reshape(block_count, tile, width)

    def exchange(x):
        return lax.all_to_all(x, AXES, 0, 0, tiled=True)

    def swap(x, mask):
        return lax.ppermute(x, AXES, [(d, d ^ mask) for d in range(devices)])

    def scattered(slots):
        return pick(ids, exchange(send_layout(slots, ids, blocks, devices)), block_count)

    def load(unit):
        at = ids // unit
        return jnp.max(jnp.sum((at[:, None] == at[None, :]).astype(jnp.int32), axis=1))

    full = (load(2 * block_count) > SLOTS) | (load(PLANE * block_count) > PLANE_SLOTS)
    most = min(stripe_count, block_count)
    spare = lax.cond(
        full,
        lambda: pick(ids, exchange(send_layout(most, ids, blocks, devices)), weight, block_count),
        lambda: jnp.zeros((stripe_count, tile // devices, width), features.dtype),
    )
    full = full.astype(jnp.int32)[None]

    keep, give = halves(ids, blocks, devices)
    sent = merge(ids, keep, swap(give, 1), block_count)
    near = [sent[0]] + [swap(x, 2 * m) for m, x in enumerate(sent) if m > 0]

    features, _ = lax.optimization_barrier((features, sent[0]))
    for_own, for_pair = listed_rows(sparse_rows[0], sparse_counts[0], features, weight)
    near[1], for_pair = lax.optimization_barrier((near[1], for_pair))
    from_pair = swap(for_pair, 1)

    near[2], spare = lax.optimization_barrier((near[2], spare))
    over = sort(ids, near, block_count)
    arrived = [over[0]] + [swap(x, PLANE * g) for g, x in enumerate(over) if g > 0]

    from_pair, _ = lax.optimization_barrier((from_pair, over[0]))
    both = jnp.stack([for_own, from_pair]).reshape(2, 2, 2, *for_own.shape[1:])
    across = swap(both[:, 1], 4)

    arrived[-1], across = lax.optimization_barrier((arrived[-1], across))

    held = choose(ids, full, arrived, spare, weight, block_count)

    parts = [held] + [swap(held, PLANE * g) for g in range(1, groups)]
    across, _ = lax.optimization_barrier((across, held))
    turned = swap(jnp.stack([both[:, 0, 1], across[:, 1]]), 2)
    listed = [both[:, 0, 0], turned[0], across[:, 0], turned[1]]
    ordered = [lax.select_n(group, *[parts[q ^ g] for g in range(groups)]) for q in range(groups)]
    own = jnp.concatenate(ordered, axis=1)

    own, *listed = lax.optimization_barrier((own, *listed))
    x, y = swap(own, 4), swap(own, 2)
    listed = [jnp.stack([r[:, g] for r in listed]) for g in range(groups)]
    listed = [swap(r, PLANE * g) if g else r for g, r in enumerate(listed)]
    half = width // 2
    left, right = swap(x[:, :, :half], 2), swap(y[:, :, half:], 4)
    pieces = [own, swap(own, 1), y, swap(y, 1), x, swap(x, 1)]
    pieces += [left, swap(left, 1), right, swap(right, 1)]

    meta = jnp.concatenate(
        [cols.reshape(-1), place ^ jnp.arange(PLANE, dtype=jnp.int32)]
    ).astype(jnp.int32)
    return layer(meta, pieces, listed, edge, sparse_w, bias.reshape(1, -1))


def solution(mesh):
    placed = (
        P(AXES, None),
        P(AXES, None, None, None),
        P(AXES, None),
        P(),
        P(AXES, None),
        P(AXES, None, None),
        P(AXES, None),
        P(),
        P(),
    )
    return jax.shard_map(
        on_device, mesh=mesh, in_specs=placed, out_specs=P(AXES, None), check_vma=False
    )
```
